512 devices in a mesh: row: 32 (over z_hi, x, y), col: 16 (over z_lo, core).
Axes of the slice: x: 4, y: 4, z: 16 (z_hi: 2, z_lo: 8; z = z_hi * 8 + z_lo), core: 2. Of those that a mesh axis runs over, the one named last changes fastest.
Arguments:
- features: bfloat16 [1024, 768, 256], P('row', 'col'), may hold values from -6 to 6
- conv_one: bfloat16 [3, 3, 256, 256], replicated, may hold values from -0.125 to 0.125
- bias_one: float32 [256], replicated, may hold values from -3 to 3
- conv_two: bfloat16 [3, 3, 256, 512], replicated, may hold values from -0.125 to 0.125
- bias_two: float32 [512], replicated, may hold values from -3 to 3
- conv_three: bfloat16 [16, 3, 3, 32, 32], P('col'), may hold values from -0.375 to 0.375
- bias_three: float32 [512], P('col'), may hold values from -3 to 3
Outputs:
- encoded: bfloat16 [512, 512, 384], P('row', 'col')
The draws below stay inside these ranges and needn't reach their ends.
All inputs are finite; a program needn't handle non-finite values.
Results may differ from the reference program's by a relative error of at most 0.0051.
Values may be sent and summed in bfloat16 or wider, within the bound.
No kernel may reach another device: no remote copies, remote signals or barrier semaphores. Data moves between devices by JAX's collectives and lax.ppermute only.
A program may use at most 64 MiB of HBM per device.

```python
import jax
import jax.numpy as jnp
from jax import lax

C1 = 256
C2 = 512
GROUPS = 16
GW = 32
H1 = 1024
W1 = 768


def block_scale(own_key, dims, pieces, low, top_value):
    level, own = 1.0, jax.random.fold_in(own_key, 6)
    for dim, parts in pieces:
        steps = jnp.exp(jax.random.uniform(jax.random.fold_in(own, dim), (parts,), jnp.float32, low / len(pieces), top_value / len(pieces)))
        level = level * jnp.repeat(steps, dims[dim] // parts).reshape([-1 if axis == dim else 1 for axis in range(len(dims))])
    return level


def gaussian(rng, shape, scale, limit, shards=(), dtype=jnp.bfloat16):
    result = scale * jax.random.normal(rng, shape, jnp.float32)
    if shards:
        result = result * block_scale(rng, shape, shards, -0.22, 0.18)
    return jnp.clip(result, -limit, limit).astype(dtype)


def setup_inputs(seed: int = 0) -> dict:
    splits = jax.random.split(jax.random.key(seed), 8)
    features = gaussian(splits[0], (H1, W1, C1), 1.0, 6.0, ((0, 32), (1, 16)))
    conv_one = gaussian(splits[1], (3, 3, C1, C1), (9 * C1) ** -0.5, 0.125)
    bias_one = gaussian(splits[2], (C1,), 0.5, 3.0, (), jnp.float32)
    conv_two = gaussian(splits[3], (3, 3, C1, C2), (9 * C1) ** -0.5, 0.125)
    bias_two = gaussian(splits[4], (C2,), 0.5, 3.0, (), jnp.float32)
    conv_three = gaussian(splits[5], (GROUPS, 3, 3, GW, GW), (9 * GW) ** -0.5, 0.375, ((0, 16),))
    bias_three = gaussian(splits[6], (C2,), 0.5, 3.0, ((0, 16),), jnp.float32)
    return {"features": features, "conv_one": conv_one, "bias_one": bias_one, "conv_two": conv_two, "bias_two": bias_two, "conv_three": conv_three, "bias_three": bias_three}


def convolve(inputs, kernel, stride, groups):
    return lax.conv_general_dilated(inputs, kernel, (stride, stride), ((1, 1), (1, 1)), dimension_numbers=("NHWC", "HWIO", "NHWC"), feature_group_count=groups, precision=lax.Precision.HIGHEST)


def reference(features, conv_one, bias_one, conv_two, bias_two, conv_three, bias_three):
    inputs = features.astype(jnp.float32)[None]
    summed = convolve(inputs, conv_one.astype(jnp.float32), 1, 1)
    layer_one = jax.nn.relu(summed + bias_one.astype(jnp.float32)).astype(jnp.bfloat16)
    summed = convolve(layer_one.astype(jnp.float32), conv_two.astype(jnp.float32), 2, 1)
    layer_two = jax.nn.relu(summed + bias_two.astype(jnp.float32)).astype(jnp.bfloat16)
    kernel = jnp.transpose(conv_three.astype(jnp.float32), (1, 2, 3, 0, 4)).reshape(3, 3, GW, GROUPS * GW)
    summed = convolve(layer_two.astype(jnp.float32), kernel, 1, GROUPS)
    summed = summed[0] + bias_three.astype(jnp.float32)
    return jnp.transpose(summed, (0, 2, 1)).astype(jnp.bfloat16)
```

```python
import functools

import jax
import jax.numpy as jnp
from jax import lax
from jax.experimental import pallas as pl
from jax.experimental.pallas import tpu as pltpu
from jax.sharding import PartitionSpec as P

BF = jnp.bfloat16
F32 = jnp.float32
ROWS, COLS, C1 = 32, 48, 256
C2, GW = 512, 32
COLS2 = COLS // 2
HALO = 4
SLAB = 208
INNER = tuple(range(0, 28, 2))
OUTER = (0, 2, 7, 9)
VMEM = pl.BlockSpec(memory_space=pltpu.VMEM)
HBM = pl.BlockSpec(memory_space=pltpu.HBM)
SMEM = pl.BlockSpec(memory_space=pltpu.SMEM)
PARAMS = pltpu.CompilerParams(vmem_limit_bytes=24 * 1024 * 1024)
LONG = pl.CostEstimate(flops=10_000_000_000, bytes_accessed=1_000_000, transcendentals=0)


def pairs_even(count):
    return [(i, i ^ 1) for i in range(count)]


def pairs_odd(count):
    return [(i, ((i + 1) ^ 1) - 1) for i in range(1, count - 1)]


def put_row(p_ref, q_ref, slot, row, left2, left1, right):
    at = lax.broadcasted_iota(jnp.int32, row.shape, 0)
    p_ref[0, slot] = jnp.where(at == 0, left1, pltpu.roll(row, 1, 0)).astype(BF)
    p_ref[1, slot] = row.astype(BF)
    p_ref[2, slot] = jnp.where(at == COLS - 1, right, pltpu.roll(row, COLS - 1, 0)).astype(BF)
    q_ref[0, slot : slot + 1] = left2
    q_ref[1, slot : slot + 1] = left1
    q_ref[2, slot : slot + 1] = row[0:1]


def two_layers(p_ref, q_ref, l_ref, w1, b1, w2, b2, count, bases, first_col, dead_rows):
    wide = -(-count // 16) * 16
    taps = [(a, b) for a in range(3) for b in range(3)]
    main = jnp.concatenate(
        [p_ref[b, a : a + count].reshape(count * COLS, C1) for a, b in taps], axis=1
    )
    edge = jnp.concatenate([q_ref[b, a : a + wide].astype(BF) for a, b in taps], axis=1)
    summed = jnp.dot(
        jnp.concatenate([main, edge], axis=0), w1[...], preferred_element_type=F32
    )
    summed = jnp.maximum(summed + b1[...], 0.0)
    for row in range(count):
        line = summed[row * COLS : (row + 1) * COLS]
        lead = jnp.where(first_col, 0.0, summed[count * COLS + row : count * COLS + row + 1])
        if row in dead_rows:
            line = jnp.where(dead_rows[row], 0.0, line)
            lead = jnp.where(dead_rows[row], 0.0, lead)
        for half in range(2):
            lanes = slice(128 * half, 128 * half + 128)
            l_ref[half, row, 8 : 8 + COLS] = line[:, lanes]
            l_ref[half, row, 7:8] = lead[:, lanes]
    windows = [
        jnp.concatenate(
            [l_ref[half, base + a, pl.ds(7 + b, COLS2, stride=2), :] for base in bases], axis=0
        ).astype(BF)
        for a, b in taps
        for half in range(2)
    ]
    summed = jnp.dot(jnp.concatenate(windows, axis=1), w2[...], preferred_element_type=F32)
    return jnp.maximum(summed + b2[...], 0.0)


def pack(layer, count, msg_ref, targets, sems):
    lane = lax.broadcasted_iota(jnp.int32, (COLS2, 128), 1) // GW
    copies = []
    for quad in range(-(-count // 4)):
        for block in range(C2 // 128):
            parts = []
            for slot in range(4):
                row = 4 * quad + slot
                if row < count:
                    part = layer[row * COLS2 : (row + 1) * COLS2, block * 128 : (block + 1) * 128]
                    parts.append([part] + [pltpu.roll(part, GW * d, 1) for d in range(1, 4)])
            for pair in range(2):
                tiles = []
                for m in (2 * pair, 2 * pair + 1):
                    tile = jnp.zeros((COLS2, 128), F32)
                    for slot, turned in enumerate(parts):
                        tile = jnp.where(lane == slot, turned[(slot - m) % 4], tile)
                    tiles.append(tile)
                at = (4 * block + 2 * pair) * COLS2
                msg_ref[quad, at : at + 2 * COLS2] = jnp.concatenate(tiles, axis=0).astype(BF)
        copies.append(pltpu.make_async_copy(msg_ref.at[quad], targets[quad], sems.at[quad]))
        copies[-1].start()
    for copy in copies:
        copy.wait()


def fill_slab(f_ref, bottom_at, left, right, out_ref, take_top):
    for k in range(HALO):
        out_ref[k * COLS : (k + 1) * COLS] = jnp.where(take_top, f_ref[k], f_ref[bottom_at + k])
    sides = [left[0], left[1], right]
    top = jnp.concatenate([s[0:HALO] for s in sides] + [left[0][0:HALO]], axis=0)
    bottom = jnp.concatenate(
        [s[ROWS - HALO : ROWS] for s in sides] + [left[0][0:HALO]], axis=0
    )
    out_ref[HALO * COLS : SLAB] = jnp.where(take_top, top, bottom).astype(BF)


def col_halo(where_ref, ca_ref, cb_ref):
    odd_col = where_ref[1] % 2 == 1
    ca = ca_ref[...].astype(F32)
    cb = cb_ref[...].astype(F32)
    return jnp.where(odd_col, ca, cb), jnp.where(odd_col, cb, ca)[0]


def col_kernel(where_ref, f_ref, sa_ref, sb_ref, edge_ref):
    for r in range(ROWS):
        low = f_ref[r, 0:16].astype(F32)
        high = f_ref[r, COLS - 16 : COLS].astype(F32)
        edge_ref[0, r : r + 1] = low[0:1]
        edge_ref[1, r : r + 1] = low[1:2]
        edge_ref[2, r : r + 1] = high[14:15]
        edge_ref[3, r : r + 1] = high[15:16]
    odd_col = where_ref[1] % 2 == 1
    first, last = edge_ref[0:2], edge_ref[2:4]
    sa_ref[...] = jnp.where(odd_col, first, last).astype(BF)
    sb_ref[...] = jnp.where(odd_col, last, first).astype(BF)


def slab_kernel(where_ref, f_ref, ca_ref, cb_ref, sa_ref, sb_ref):
    odd_row = where_ref[0] % 2 == 1
    left, right = col_halo(where_ref, ca_ref, cb_ref)
    fill_slab(f_ref, ROWS - HALO, left, right, sa_ref, odd_row)
    fill_slab(f_ref, ROWS - HALO, left, right, sb_ref, jnp.logical_not(odd_row))


def inner_kernel(
    where_ref, f_ref, ca_ref, cb_ref, w1, b1, w2, b2, out_ref, msg_ref, p_ref, q_ref, l_ref, sems
):
    q_ref[...] = jnp.zeros_like(q_ref)
    left, right = col_halo(where_ref, ca_ref, cb_ref)
    for r in range(31):
        put_row(
            p_ref, q_ref, r, f_ref[r].astype(F32),
            left[0, r : r + 1], left[1, r : r + 1], right[r : r + 1],
        )
    layer = two_layers(
        p_ref, q_ref, l_ref, w1, b1, w2, b2, 29, INNER, where_ref[1] == 0, {}
    )
    pack(layer, 14, msg_ref, [out_ref.at[:, 128 * q : 128 * q + 128] for q in range(4)], sems)


def outer_kernel(
    where_ref, ca_ref, cb_ref, rb_ref, ra_ref, w1, b1, w2, b2, f_ref, inner_hbm,
    out_ref, msg_ref, p_ref, q_ref, l_ref, sems,
):
    del inner_hbm
    q_ref[...] = jnp.zeros_like(q_ref)
    odd_row = where_ref[0] % 2 == 1
    first = where_ref[0] == 0
    last = where_ref[0] == where_ref[2] - 1
    left, right = col_halo(where_ref, ca_ref, cb_ref)

    def own(slot, r):
        put_row(
            p_ref, q_ref, slot, f_ref[r].astype(F32),
            left[0, r : r + 1], left[1, r : r + 1], right[r : r + 1],
        )

    ra_end = ra_ref[HALO * COLS : SLAB].astype(F32)
    rb_end = rb_ref[HALO * COLS : SLAB].astype(F32)

    def halo(slot, k, from_a):
        a = ra_ref[k * COLS : (k + 1) * COLS]
        b = rb_ref[k * COLS : (k + 1) * COLS]
        row = jnp.where(from_a, a, b).astype(F32)
        end = jnp.where(from_a, ra_end, rb_end)
        put_row(
            p_ref, q_ref, slot, row,
            end[k : k + 1], end[HALO + k : HALO + k + 1], end[2 * HALO + k : 2 * HALO + k + 1],
        )

    for k in range(4):
        halo(k, k, odd_row)
    for k in range(3):
        halo(11 + k, k, jnp.logical_not(odd_row))
    for k in range(3):
        own(4 + k, k)
    for k in range(4):
        own(7 + k, ROWS - 4 + k)
    dead = {0: first, 1: first, 2: first, 10: last, 11: last}
    layer = two_layers(
        p_ref, q_ref, l_ref, w1, b1, w2, b2, 12, OUTER, where_ref[1] == 0, dead
    )
    at = lax.broadcasted_iota(jnp.int32, layer.shape, 0) // COLS2
    gone = jnp.logical_or(
        jnp.logical_and(at == 0, first), jnp.logical_and(at == 3, last)
    )
    pack(jnp.where(gone, 0.0, layer), 4, msg_ref, [out_ref.at[:, 512:640]], sems)


LOW = tuple(range(1, 9)) + (-1, 0, 15, 16)
HIGH = tuple(range(5, 15)) + (None, None, -1, 0, 15, 16)


def spread_kernel(w_ref, low_ref, high_ref):
    shape = (GW, 8 * GW)
    turn = lax.broadcasted_iota(jnp.int32, shape, 1) % GW == lax.broadcasted_iota(jnp.int32, shape, 0)
    wide = jnp.dot(w_ref[...], turn.astype(BF), preferred_element_type=F32)
    lane = lax.broadcasted_iota(jnp.int32, shape, 1) // GW
    for half, (rows, ref) in enumerate(((LOW, low_ref), (HIGH, high_ref))):
        for b in range(3):
            for slot, row in enumerate(rows):
                tile = jnp.zeros(shape, F32)
                for a in range(3):
                    out = None if row is None else row + 1 - a - 8 * half
                    if out is not None and 0 <= out < 8:
                        at = (3 * a + b) * GW
                        tile = jnp.where(lane == out, wide[at : at + GW], tile)
                ref[b, slot * GW : (slot + 1) * GW] = tile.astype(BF)


def grouped_kernel(x_ref, low_ref, high_ref, bias_ref, out_ref):
    cols = x_ref.shape[0]
    at = lax.broadcasted_iota(jnp.int32, (cols, 8 * GW), 0)
    for half, (lanes, ref) in enumerate(((slice(0, 256), low_ref), (slice(128, 512), high_ref))):
        x = jnp.concatenate([x_ref[:, lanes], x_ref[:, 512:640]], axis=1)
        before, here, after = (
            jnp.dot(x, ref[b], preferred_element_type=F32) for b in range(3)
        )
        total = here + bias_ref[...]
        total = total + jnp.where(at == 0, 0.0, pltpu.roll(before, 1, 0))
        total = total + jnp.where(at == cols - 1, 0.0, pltpu.roll(after, cols - 1, 0))
        out_ref[half * 256 : (half + 1) * 256] = total.T.astype(BF)


def on_device(features, conv_one, bias_one, conv_two, bias_two, conv_three, bias_three):
    row, col = lax.axis_index("row"), lax.axis_index("col")
    row_count, col_count = lax.axis_size("row"), lax.axis_size("col")
    where = jnp.stack([row, col, jnp.int32(row_count)]).astype(jnp.int32)
    low, high = pl.pallas_call(
        spread_kernel,
        out_shape=(
            jax.ShapeDtypeStruct((3, len(LOW) * GW, 8 * GW), BF),
            jax.ShapeDtypeStruct((3, len(HIGH) * GW, 8 * GW), BF),
        ),
        in_specs=[VMEM],
        out_specs=(VMEM, VMEM),
        compiler_params=PARAMS,
        name="spread_weights",
    )(conv_three.reshape(9 * GW, GW))
    w1, b1 = conv_one.reshape(9 * C1, C1), bias_one.reshape(1, C1)
    w2, b2 = conv_two.reshape(9 * C1, C2), bias_two.reshape(1, C2)
    b3 = jnp.tile(bias_three, 8).reshape(1, 8 * GW)

    edge = jax.ShapeDtypeStruct((2, ROWS, C1), BF)
    ca, cb = pl.pallas_call(
        col_kernel,
        out_shape=(edge, edge),
        in_specs=[SMEM, VMEM],
        out_specs=(VMEM, VMEM),
        scratch_shapes=[pltpu.VMEM((4, ROWS, C1), F32)],
        compiler_params=PARAMS,
        cost_estimate=LONG,
        name="col_edges",
    )(where, features)
    ca = lax.ppermute(ca, "col", pairs_even(col_count))
    cb = lax.ppermute(cb, "col", pairs_odd(col_count))

    slab = jax.ShapeDtypeStruct((SLAB, C1), BF)
    message = jax.ShapeDtypeStruct((16 * COLS2, 640), BF)
    sa, sb = pl.pallas_call(
        slab_kernel,
        out_shape=(slab, slab),
        in_specs=[SMEM, VMEM, VMEM, VMEM],
        out_specs=(VMEM, VMEM),
        compiler_params=PARAMS,
        cost_estimate=LONG,
        name="row_slabs",
    )(where, features, ca, cb)
    ra = lax.ppermute(sa, "row", pairs_even(row_count))
    rb = lax.ppermute(sb, "row", pairs_odd(row_count))
    inner = pl.pallas_call(
        inner_kernel,
        out_shape=message,
        in_specs=[SMEM] + [VMEM] * 7,
        out_specs=HBM,
        scratch_shapes=[
            pltpu.VMEM((4, 16 * COLS2, 128), BF),
            pltpu.VMEM((3, 31, COLS, C1), BF),
            pltpu.VMEM((3, 40, C1), F32),
            pltpu.VMEM((2, 29, 56, 128), F32),
            pltpu.SemaphoreType.DMA((4,)),
        ],
        compiler_params=PARAMS,
        cost_estimate=pl.CostEstimate(
            flops=2 * 9 * C1 * (29 * 48 * C1 + 14 * 24 * C2), bytes_accessed=6_000_000, transcendentals=0
        ),
        name="inner_rows",
    )(where, features, ca, cb, w1, b1, w2, b2)
    sent = pl.pallas_call(
        outer_kernel,
        out_shape=message,
        in_specs=[SMEM] + [VMEM] * 9 + [HBM],
        out_specs=HBM,
        input_output_aliases={10: 0},
        scratch_shapes=[
            pltpu.VMEM((1, 16 * COLS2, 128), BF),
            pltpu.VMEM((3, 14, COLS, C1), BF),
            pltpu.VMEM((3, 24, C1), F32),
            pltpu.VMEM((2, 12, 56, 128), F32),
            pltpu.SemaphoreType.DMA((1,)),
        ],
        compiler_params=PARAMS,
        cost_estimate=pl.CostEstimate(
            flops=2 * 9 * C1 * (12 * 48 * C1 + 4 * 24 * C2), bytes_accessed=4_000_000, transcendentals=0
        ),
        name="outer_rows",
    )(where, ca, cb, rb, ra, w1, b1, w2, b2, features, inner)
    x = lax.all_to_all(sent.reshape(16, COLS2, 640), "col", 0, 0, tiled=True)
    out = pl.pallas_call(
        grouped_kernel,
        out_shape=jax.ShapeDtypeStruct((16 * GW, 16 * COLS2), BF),
        in_specs=[VMEM] * 4,
        out_specs=VMEM,
        compiler_params=PARAMS,
        name="grouped",
    )(x.reshape(16 * COLS2, 640), low, high, b3)
    return out.reshape(16, GW, 16 * COLS2)


def solution(mesh):
    in_specs = (
        P("row", "col", None),
        P(),
        P(),
        P(),
        P(),
        P("col", None, None, None, None),
        P("col"),
    )
    out_specs = P("row", "col", None)
    return jax.shard_map(
        on_device, mesh=mesh, in_specs=in_specs, out_specs=out_specs, check_vma=False
    )
```

```python
import functools

import jax
import jax.numpy as jnp
from jax import lax
from jax.experimental import pallas as pl
from jax.experimental.pallas import tpu as pltpu
from jax.sharding import PartitionSpec as P

BF = jnp.bfloat16
F32 = jnp.float32
ROWS, COLS, C1 = 32, 48, 256
C2, GW = 512, 32
COLS2 = COLS // 2
HALO = 4
SLAB = 208
INNER = tuple(range(0, 28, 2))
DEPTH = 112
VMEM = pl.BlockSpec(memory_space=pltpu.VMEM)
HBM = pl.BlockSpec(memory_space=pltpu.HBM)
SMEM = pl.BlockSpec(memory_space=pltpu.SMEM)
PARAMS = pltpu.CompilerParams(vmem_limit_bytes=24 * 1024 * 1024)
LONG = pl.CostEstimate(flops=10_000_000_000, bytes_accessed=1_000_000, transcendentals=0)


def pairs_even(count):
    return [(i, i ^ 1) for i in range(count)]


def pairs_odd(count):
    return [(i, ((i + 1) ^ 1) - 1) for i in range(1, count - 1)]


def put_row(p_ref, q_ref, slot, row, left2, left1, right):
    at = lax.broadcasted_iota(jnp.int32, row.shape, 0)
    p_ref[0, slot] = jnp.where(at == 0, left1, pltpu.roll(row, 1, 0)).astype(BF)
    p_ref[1, slot] = row.astype(BF)
    p_ref[2, slot] = jnp.where(at == COLS - 1, right, pltpu.roll(row, COLS - 1, 0)).astype(BF)
    q_ref[0, slot : slot + 1] = left2
    q_ref[1, slot : slot + 1] = left1
    q_ref[2, slot : slot + 1] = row[0:1]


def layer_one(p_ref, q_ref, l_ref, w1, b1, spans, first_col, dead_rows):
    total = sum(count for _, count, _ in spans)
    wide = -(-total // 16) * 16
    taps = [(a, b) for a in range(3) for b in range(3)]
    main = jnp.concatenate(
        [
            jnp.concatenate(
                [p_ref[b, at + a : at + a + count].reshape(count * COLS, C1) for a, b in taps], axis=1
            )
            for at, count, _ in spans
        ],
        axis=0,
    )
    rest = [jnp.zeros((wide - total, C1), F32)] if wide > total else []
    edge = jnp.concatenate(
        [
            jnp.concatenate(
                [q_ref[b, at + a : at + a + count] for at, count, _ in spans] + rest, axis=0
            ).astype(BF)
            for a, b in taps
        ],
        axis=1,
    )
    summed = jnp.dot(
        jnp.concatenate([main, edge], axis=0), w1[...], preferred_element_type=F32
    )
    summed = jnp.maximum(summed + b1[...], 0.0)
    done = 0
    for _, count, to in spans:
        for row in range(to, to + count):
            line = summed[done * COLS : (done + 1) * COLS]
            lead = summed[total * COLS + done : total * COLS + done + 1]
            lead = jnp.where(first_col, 0.0, lead)
            if row in dead_rows:
                line = jnp.where(dead_rows[row], 0.0, line)
                lead = jnp.where(dead_rows[row], 0.0, lead)
            for half in range(2):
                lanes = slice(128 * half, 128 * half + 128)
                l_ref[half, row, 8 : 8 + COLS] = line[:, lanes]
                l_ref[half, row, 7:8] = lead[:, lanes]
            done += 1


def layer_two(l_ref, w2, b2, bases):
    windows = [
        jnp.concatenate(
            [l_ref[half, base + a, pl.ds(7 + b, COLS2, stride=2), :] for base in bases], axis=0
        ).astype(BF)
        for a in range(3)
        for b in range(3)
        for half in range(2)
    ]
    summed = jnp.dot(jnp.concatenate(windows, axis=1), w2[...], preferred_element_type=F32)
    return jnp.maximum(summed + b2[...], 0.0)


def quad_tiles(layer, rows):
    lane = lax.broadcasted_iota(jnp.int32, (COLS2, 128), 1) // GW
    tiles = []
    for block in range(C2 // 128):
        turned = {}
        for slot, row in enumerate(rows):
            if row is not None:
                part = layer[row * COLS2 : (row + 1) * COLS2, block * 128 : (block + 1) * 128]
                turned[slot] = [part] + [pltpu.roll(part, GW * d, 1) for d in range(1, 4)]
        for m in range(4):
            tile = jnp.zeros((COLS2, 128), F32)
            for slot, parts in turned.items():
                tile = jnp.where(lane == slot, parts[(slot - m) % 4], tile)
            tiles.append(tile)
    return tiles


def fill_slab(f_ref, bottom_at, left, right, out_ref, take_top):
    for k in range(HALO):
        out_ref[k * COLS : (k + 1) * COLS] = jnp.where(take_top, f_ref[k], f_ref[bottom_at + k])
    sides = [left[0], left[1], right]
    top = jnp.concatenate([s[0:HALO] for s in sides] + [left[0][0:HALO]], axis=0)
    bottom = jnp.concatenate(
        [s[ROWS - HALO : ROWS] for s in sides] + [left[0][0:HALO]], axis=0
    )
    out_ref[HALO * COLS : SLAB] = jnp.where(take_top, top, bottom).astype(BF)


def col_halo(where_ref, ca_ref, cb_ref):
    odd_col = where_ref[1] % 2 == 1
    ca = ca_ref[...].astype(F32)
    cb = cb_ref[...].astype(F32)
    return jnp.where(odd_col, ca, cb), jnp.where(odd_col, cb, ca)[0]


def col_kernel(where_ref, f_ref, sa_ref, sb_ref, edge_ref):
    for r in range(ROWS):
        low = f_ref[r, 0:16].astype(F32)
        high = f_ref[r, COLS - 16 : COLS].astype(F32)
        edge_ref[0, r : r + 1] = low[0:1]
        edge_ref[1, r : r + 1] = low[1:2]
        edge_ref[2, r : r + 1] = high[14:15]
        edge_ref[3, r : r + 1] = high[15:16]
    odd_col = where_ref[1] % 2 == 1
    first, last = edge_ref[0:2], edge_ref[2:4]
    sa_ref[...] = jnp.where(odd_col, first, last).astype(BF)
    sb_ref[...] = jnp.where(odd_col, last, first).astype(BF)


def slab_kernel(where_ref, f_ref, cb_ref, ca_ref, sa_ref, sb_ref):
    odd_row = where_ref[0] % 2 == 1
    left, right = col_halo(where_ref, ca_ref, cb_ref)
    fill_slab(f_ref, ROWS - HALO, left, right, sa_ref, odd_row)
    fill_slab(f_ref, ROWS - HALO, left, right, sb_ref, jnp.logical_not(odd_row))


def inner_kernel(
    where_ref, f_ref, cb_ref, ca_ref, w1, b1, w2, b2,
    out_ref, tail_ref, rim_ref, msg_ref, p_ref, q_ref, l_ref, sem,
):
    left, right = col_halo(where_ref, ca_ref, cb_ref)
    for r in range(31):
        put_row(
            p_ref, q_ref, r, f_ref[r].astype(F32),
            left[0, r : r + 1], left[1, r : r + 1], right[r : r + 1],
        )
    layer_one(p_ref, q_ref, l_ref, w1, b1, ((0, 29, 0),), where_ref[1] == 0, {})
    rim_ref[:, 0] = l_ref[:, 0]
    rim_ref[:, 1] = l_ref[:, 28]
    layer = layer_two(l_ref, w2, b2, INNER)
    tiles = zip(quad_tiles(layer, (0, 1, 2, 3)), quad_tiles(layer, (4, 5, 6, 7)), strict=True)
    for group, pair in enumerate(tiles):
        msg_ref[group] = jnp.concatenate(pair, axis=0).astype(BF)
    copy = pltpu.make_async_copy(msg_ref, out_ref.at[:, 0:48], sem)
    copy.start()
    tiles = zip(
        quad_tiles(layer, (8, 9, 10, 11)), quad_tiles(layer, (12, 13, None, None)), strict=True
    )
    for group, pair in enumerate(tiles):
        tail_ref[group] = jnp.concatenate(pair, axis=0).astype(BF)
    copy.wait()


def side_rows(
    where_ref, cb_ref, ca_ref, r_ref, w1, b1, w2, b2, f_ref, rim_ref, p_ref, q_ref, l_ref, is_top
):
    left, right = col_halo(where_ref, ca_ref, cb_ref)
    end = r_ref[HALO * COLS : SLAB].astype(F32)

    def own(r):
        return (
            f_ref[r].astype(F32), left[0, r : r + 1], left[1, r : r + 1], right[r : r + 1]
        )

    def halo(k):
        return (
            r_ref[k * COLS : (k + 1) * COLS].astype(F32),
            end[k : k + 1], end[HALO + k : HALO + k + 1], end[2 * HALO + k : 2 * HALO + k + 1],
        )

    above = [halo(k) for k in range(4)] + [own(0), own(1)]
    below = [own(ROWS - 3 + k) for k in range(3)] + [halo(k) for k in range(3)]
    for slot, (top, bottom) in enumerate(zip(above, below, strict=True)):
        parts = [jnp.where(is_top, x, y) for x, y in zip(top, bottom, strict=True)]
        put_row(p_ref, q_ref, slot, *parts)
    l_ref[:, 0] = rim_ref[:, 1]
    l_ref[:, 5] = rim_ref[:, 0]
    off_top = jnp.logical_and(is_top, where_ref[0] == 0)
    off_bottom = jnp.logical_and(jnp.logical_not(is_top), where_ref[0] == where_ref[2] - 1)
    dead = {1: off_top, 2: off_top, 3: jnp.logical_or(off_top, off_bottom), 4: off_bottom}
    layer_one(p_ref, q_ref, l_ref, w1, b1, ((0, 4, 1),), where_ref[1] == 0, dead)
    base = jnp.where(is_top, 1, 0)
    layer = layer_two(l_ref, w2, b2, (base, base + 2))
    at = lax.broadcasted_iota(jnp.int32, layer.shape, 0) // COLS2
    gone = jnp.logical_or(
        jnp.logical_and(at == 0, off_top), jnp.logical_and(at == 1, off_bottom)
    )
    return jnp.where(gone, 0.0, layer)


def even_kernel(
    where_ref, cb_ref, ca_ref, ra_ref, w1, b1, w2, b2, f_ref, rim_ref, tail_ref, inner_hbm,
    out_ref, msg_ref, p_ref, q_ref, l_ref, sem,
):
    del inner_hbm
    layer = side_rows(
        where_ref, cb_ref, ca_ref, ra_ref, w1, b1, w2, b2, f_ref, rim_ref, p_ref, q_ref, l_ref,
        where_ref[0] % 2 == 1,
    )
    for group, tile in enumerate(quad_tiles(layer, (None, None, 0, 1))):
        tail = tail_ref[group].astype(F32)
        msg_ref[group] = jnp.concatenate(
            [tail[0:COLS2], tail[COLS2:] + tile], axis=0
        ).astype(BF)
    copy = pltpu.make_async_copy(msg_ref, out_ref.at[:, 48:96], sem)
    copy.start()
    copy.wait()


def odd_kernel(
    where_ref, cb_ref, ca_ref, rb_ref, w1, b1, w2, b2, f_ref, rim_ref, inner_hbm,
    out_ref, msg_ref, p_ref, q_ref, l_ref, sem,
):
    del inner_hbm
    layer = side_rows(
        where_ref, cb_ref, ca_ref, rb_ref, w1, b1, w2, b2, f_ref, rim_ref, p_ref, q_ref, l_ref,
        where_ref[0] % 2 == 0,
    )
    low = lax.broadcasted_iota(jnp.int32, (COLS2, 128), 1) < 64
    for group, tile in enumerate(quad_tiles(layer, (0, 1, None, None))):
        folded = pltpu.roll(pltpu.roll(tile, 64, 1), COLS2 // 2, 0)
        msg_ref[group] = jnp.where(low, tile, folded)[0:16].astype(BF)
    copy = pltpu.make_async_copy(msg_ref, out_ref.at[:, 96:DEPTH], sem)
    copy.start()
    copy.wait()


LOW = tuple(tuple(range(1, 9)) + (13, 14) + end for end in ((15, 16, -1, 0), (-1, 0, 15, 16)))
HIGH = tuple(tuple(range(5, 15)) + end for end in ((15, 16, -1, 0), (-1, 0, 15, 16)))
SLOTS = 16


def spread_kernel(where_ref, w_ref, low_ref, high_ref):
    shape = (GW, 8 * GW)
    turn = lax.broadcasted_iota(jnp.int32, shape, 1) % GW == lax.broadcasted_iota(jnp.int32, shape, 0)
    wide = jnp.dot(w_ref[...], turn.astype(BF), preferred_element_type=F32)
    lane = lax.broadcasted_iota(jnp.int32, shape, 1) // GW
    odd_row = where_ref[0] % 2 == 1

    def band(row, b, half):
        tile = jnp.zeros(shape, F32)
        for a in range(3):
            out = row + 1 - a - 8 * half
            if 0 <= out < 8:
                at = (3 * a + b) * GW
                tile = jnp.where(lane == out, wide[at : at + GW], tile)
        return tile

    for half, (rows, ref) in enumerate(((LOW, low_ref), (HIGH, high_ref))):
        for b in range(3):
            for slot, (even, odd) in enumerate(zip(*rows, strict=True)):
                tile = band(even, b, half)
                if even != odd:
                    tile = jnp.where(odd_row, band(odd, b, half), tile)
                ref[b, slot * GW : (slot + 1) * GW] = tile.astype(BF)
            ref[b, len(rows[0]) * GW :] = jnp.zeros(((SLOTS - len(rows[0])) * GW, 8 * GW), BF)


def grouped_kernel(x_ref, low_ref, high_ref, bias_ref, out_ref, held_ref, res_ref, sems):
    groups = x_ref.shape[0]
    cols = groups * COLS2
    half_row = lax.broadcasted_iota(jnp.int32, (COLS2, 128), 0) < COLS2 // 2
    for pair in range(groups // 2):
        blocks = [[] for _ in range(5)]
        for source in (2 * pair, 2 * pair + 1):
            held = x_ref[source].astype(F32)
            for quad in range(4):
                blocks[quad].append(held[quad * COLS2 : (quad + 1) * COLS2])
            folded = jnp.concatenate([held[96:DEPTH], held[96:104]], axis=0)
            turned = pltpu.roll(pltpu.roll(folded, 64, 1), COLS2 // 2, 0)
            blocks[4].append(jnp.where(half_row, folded, turned))
        for quad, parts in enumerate(blocks):
            held_ref[pair * 2 * COLS2 : (pair + 1) * 2 * COLS2, quad * 128 : (quad + 1) * 128] = (
                jnp.concatenate(parts, axis=0).astype(BF)
            )
    at = lax.broadcasted_iota(jnp.int32, (cols, 8 * GW), 0)
    copies = []
    for half, ref in enumerate((low_ref, high_ref)):
        if half == 0:
            x = jnp.concatenate([held_ref[:, 0:256], held_ref[:, 384:640]], axis=1)
        else:
            x = held_ref[:, 128:640]
        before, here, after = (
            jnp.dot(x, ref[b], preferred_element_type=F32) for b in range(3)
        )
        total = here + bias_ref[...]
        total = total + jnp.where(at == 0, 0.0, pltpu.roll(before, 1, 0))
        total = total + jnp.where(at == cols - 1, 0.0, pltpu.roll(after, cols - 1, 0))
        res_ref[half] = total.T.astype(BF)
        copies.append(
            pltpu.make_async_copy(res_ref.at[half], out_ref.at[256 * half : 256 * half + 256], sems.at[half])
        )
        copies[-1].start()
    for copy in copies:
        copy.wait()


def on_device(features, conv_one, bias_one, conv_two, bias_two, conv_three, bias_three):
    row, col = lax.axis_index("row"), lax.axis_index("col")
    row_count, col_count = lax.axis_size("row"), lax.axis_size("col")
    where = jnp.stack([row, col, jnp.int32(row_count)]).astype(jnp.int32)
    low, high = pl.pallas_call(
        spread_kernel,
        out_shape=(
            jax.ShapeDtypeStruct((3, SLOTS * GW, 8 * GW), BF),
            jax.ShapeDtypeStruct((3, SLOTS * GW, 8 * GW), BF),
        ),
        in_specs=[SMEM, VMEM],
        out_specs=(VMEM, VMEM),
        compiler_params=PARAMS,
        name="spread_weights",
    )(where, conv_three.reshape(9 * GW, GW))
    w1, b1 = conv_one.reshape(9 * C1, C1), bias_one.reshape(1, C1)
    w2, b2 = conv_two.reshape(9 * C1, C2), bias_two.reshape(1, C2)
    b3 = jnp.tile(bias_three, 8).reshape(1, 8 * GW)

    edge = jax.ShapeDtypeStruct((2, ROWS, C1), BF)
    ca, cb = pl.pallas_call(
        col_kernel,
        out_shape=(edge, edge),
        in_specs=[SMEM, VMEM],
        out_specs=(VMEM, VMEM),
        scratch_shapes=[pltpu.VMEM((4, ROWS, C1), F32)],
        compiler_params=PARAMS,
        cost_estimate=LONG,
        name="col_edges",
    )(where, features)
    ca = lax.ppermute(ca, "col", pairs_even(col_count))
    cb = lax.ppermute(cb, "col", pairs_odd(col_count))

    slab = jax.ShapeDtypeStruct((SLAB, C1), BF)
    message = jax.ShapeDtypeStruct((16, DEPTH, 128), BF)
    sa, sb = pl.pallas_call(
        slab_kernel,
        out_shape=(slab, slab),
        in_specs=[SMEM, VMEM, VMEM, VMEM],
        out_specs=(VMEM, VMEM),
        compiler_params=PARAMS,
        cost_estimate=LONG,
        name="row_slabs",
    )(where, features, cb, ca)
    ra = lax.ppermute(sa, "row", pairs_even(row_count))
    rb = lax.ppermute(sb, "row", pairs_odd(row_count))
    inner, tail, rim = pl.pallas_call(
        inner_kernel,
        out_shape=(
            message,
            jax.ShapeDtypeStruct((16, 48, 128), BF),
            jax.ShapeDtypeStruct((2, 2, 56, 128), F32),
        ),
        in_specs=[SMEM] + [VMEM] * 7,
        out_specs=(HBM, VMEM, VMEM),
        scratch_shapes=[
            pltpu.VMEM((16, 48, 128), BF),
            pltpu.VMEM((3, 31, COLS, C1), BF),
            pltpu.VMEM((3, 32, C1), F32),
            pltpu.VMEM((2, 29, 56, 128), F32),
            pltpu.SemaphoreType.DMA,
        ],
        compiler_params=PARAMS,
        cost_estimate=pl.CostEstimate(
            flops=2 * 9 * C1 * (29 * 48 * C1 + 14 * 24 * C2), bytes_accessed=6_000_000, transcendentals=0
        ),
        name="inner_rows",
    )(where, features, cb, ca, w1, b1, w2, b2)
    sides = [
        pltpu.VMEM((3, 6, COLS, C1), BF),
        pltpu.VMEM((3, 8, C1), F32),
        pltpu.VMEM((2, 6, 56, 128), F32),
        pltpu.SemaphoreType.DMA,
    ]
    cost = pl.CostEstimate(
        flops=2 * 9 * C1 * (4 * 48 * C1 + 2 * 24 * C2), bytes_accessed=4_000_000, transcendentals=0
    )
    sent = pl.pallas_call(
        even_kernel,
        out_shape=message,
        in_specs=[SMEM] + [VMEM] * 10 + [HBM],
        out_specs=HBM,
        input_output_aliases={11: 0},
        scratch_shapes=[pltpu.VMEM((16, 48, 128), BF)] + sides,
        compiler_params=PARAMS,
        cost_estimate=cost,
        name="even_side",
    )(where, cb, ca, ra, w1, b1, w2, b2, features, rim, tail, inner)
    sent = pl.pallas_call(
        odd_kernel,
        out_shape=message,
        in_specs=[SMEM] + [VMEM] * 9 + [HBM],
        out_specs=HBM,
        input_output_aliases={10: 0},
        scratch_shapes=[pltpu.VMEM((16, 16, 128), BF)] + sides,
        compiler_params=PARAMS,
        cost_estimate=cost,
        name="odd_side",
    )(where, cb, ca, rb, w1, b1, w2, b2, features, rim, sent)
    x = lax.all_to_all(sent, "col", 0, 0, tiled=True)
    out = pl.pallas_call(
        grouped_kernel,
        out_shape=jax.ShapeDtypeStruct((16 * GW, 16 * COLS2), BF),
        in_specs=[VMEM] * 4,
        out_specs=HBM,
        scratch_shapes=[
            pltpu.VMEM((16 * COLS2, 640), BF),
            pltpu.VMEM((2, 8 * GW, 16 * COLS2), BF),
            pltpu.SemaphoreType.DMA((2,)),
        ],
        compiler_params=PARAMS,
        name="grouped",
    )(x, low, high, b3)
    return out.reshape(16, GW, 16 * COLS2)


def solution(mesh):
    in_specs = (
        P("row", "col", None),
        P(),
        P(),
        P(),
        P(),
        P("col", None, None, None, None),
        P("col"),
    )
    out_specs = P("row", "col", None)
    return jax.shard_map(
        on_device, mesh=mesh, in_specs=in_specs, out_specs=out_specs, check_vma=False
    )
```

```python
import functools

import jax
import jax.numpy as jnp
from jax import lax
from jax.experimental import pallas as pl
from jax.experimental.pallas import tpu as pltpu
from jax.sharding import PartitionSpec as P

BF = jnp.bfloat16
F32 = jnp.float32
ROWS, COLS, C1 = 32, 48, 256
C2, GW = 512, 32
COLS2 = COLS // 2
HALO = 4
SLAB = 208
INNER = tuple(range(0, 28, 2))
DEPTH = 112
VMEM = pl.BlockSpec(memory_space=pltpu.VMEM)
HBM = pl.BlockSpec(memory_space=pltpu.HBM)
SMEM = pl.BlockSpec(memory_space=pltpu.SMEM)
PARAMS = pltpu.CompilerParams(vmem_limit_bytes=24 * 1024 * 1024)
LONG = pl.CostEstimate(flops=10_000_000_000, bytes_accessed=1_000_000, transcendentals=0)


def pairs_even(count):
    return [(i, i ^ 1) for i in range(count)]


def pairs_odd(count):
    return [(i, ((i + 1) ^ 1) - 1) for i in range(1, count - 1)]


def put_row(p_ref, q_ref, slot, row, left2, left1, right):
    at = lax.broadcasted_iota(jnp.int32, row.shape, 0)
    p_ref[0, slot] = jnp.where(at == 0, left1, pltpu.roll(row, 1, 0)).astype(BF)
    p_ref[1, slot] = row.astype(BF)
    p_ref[2, slot] = jnp.where(at == COLS - 1, right, pltpu.roll(row, COLS - 1, 0)).astype(BF)
    q_ref[0, slot : slot + 1] = left2
    q_ref[1, slot : slot + 1] = left1
    q_ref[2, slot : slot + 1] = row[0:1]


def layer_one(p_ref, q_ref, l_ref, w1, b1, spans, first_col, dead_rows):
    total = sum(count for _, count, _ in spans)
    wide = -(-total // 16) * 16
    taps = [(a, b) for a in range(3) for b in range(3)]
    main = jnp.concatenate(
        [
            jnp.concatenate(
                [p_ref[b, at + a : at + a + count].reshape(count * COLS, C1) for a, b in taps], axis=1
            )
            for at, count, _ in spans
        ],
        axis=0,
    )
    rest = [jnp.zeros((wide - total, C1), F32)] if wide > total else []
    edge = jnp.concatenate(
        [
            jnp.concatenate(
                [q_ref[b, at + a : at + a + count] for at, count, _ in spans] + rest, axis=0
            ).astype(BF)
            for a, b in taps
        ],
        axis=1,
    )
    summed = jnp.dot(
        jnp.concatenate([main, edge], axis=0), w1[...], preferred_element_type=F32
    )
    summed = jnp.maximum(summed + b1[...], 0.0)
    done = 0
    for _, count, to in spans:
        for row in range(to, to + count):
            line = summed[done * COLS : (done + 1) * COLS]
            lead = summed[total * COLS + done : total * COLS + done + 1]
            lead = jnp.where(first_col, 0.0, lead)
            if row in dead_rows:
                line = jnp.where(dead_rows[row], 0.0, line)
                lead = jnp.where(dead_rows[row], 0.0, lead)
            for half in range(2):
                lanes = slice(128 * half, 128 * half + 128)
                l_ref[half, row, 8 : 8 + COLS] = line[:, lanes]
                l_ref[half, row, 7:8] = lead[:, lanes]
            done += 1


def layer_two(l_ref, w2, b2, bases):
    windows = [
        jnp.concatenate(
            [l_ref[half, base + a, pl.ds(7 + b, COLS2, stride=2), :] for base in bases], axis=0
        ).astype(BF)
        for a in range(3)
        for b in range(3)
        for half in range(2)
    ]
    summed = jnp.dot(jnp.concatenate(windows, axis=1), w2[...], preferred_element_type=F32)
    return jnp.maximum(summed + b2[...], 0.0)


def quad_tiles(layer, rows):
    lane = lax.broadcasted_iota(jnp.int32, (COLS2, 128), 1) // GW
    tiles = []
    for block in range(C2 // 128):
        turned = {}
        for slot, row in enumerate(rows):
            if row is not None:
                part = layer[row * COLS2 : (row + 1) * COLS2, block * 128 : (block + 1) * 128]
                turned[slot] = [part] + [pltpu.roll(part, GW * d, 1) for d in range(1, 4)]
        for m in range(4):
            tile = jnp.zeros((COLS2, 128), F32)
            for slot, parts in turned.items():
                tile = jnp.where(lane == slot, parts[(slot - m) % 4], tile)
            tiles.append(tile)
    return tiles


def fill_slab(f_ref, bottom_at, left, right, out_ref, take_top):
    for k in range(HALO):
        out_ref[k * COLS : (k + 1) * COLS] = jnp.where(take_top, f_ref[k], f_ref[bottom_at + k])
    sides = [left[0], left[1], right]
    top = jnp.concatenate([s[0:HALO] for s in sides] + [left[0][0:HALO]], axis=0)
    bottom = jnp.concatenate(
        [s[ROWS - HALO : ROWS] for s in sides] + [left[0][0:HALO]], axis=0
    )
    out_ref[HALO * COLS : SLAB] = jnp.where(take_top, top, bottom).astype(BF)


def col_halo(where_ref, ca_ref, cb_ref):
    odd_col = where_ref[1] % 2 == 1
    ca = ca_ref[...].astype(F32)
    cb = cb_ref[...].astype(F32)
    return jnp.where(odd_col, ca, cb), jnp.where(odd_col, cb, ca)[0]


def parity_kernel(where_ref, out_ref):
    out_ref[...] = jnp.full(out_ref.shape, where_ref[0] % 2, jnp.int32)


def slab_kernel(where_ref, f_ref, cb_ref, ca_ref, parity_ref, sa_ref, sb_ref):
    del parity_ref
    odd_row = where_ref[0] % 2 == 1
    left, right = col_halo(where_ref, ca_ref, cb_ref)
    fill_slab(f_ref, ROWS - HALO, left, right, sa_ref, odd_row)
    fill_slab(f_ref, ROWS - HALO, left, right, sb_ref, jnp.logical_not(odd_row))


def inner_kernel(
    where_ref, f_ref, cb_ref, ca_ref, w1, b1, w2, b2,
    out_ref, tail_ref, rim_ref, msg_ref, p_ref, q_ref, l_ref, sem,
):
    left, right = col_halo(where_ref, ca_ref, cb_ref)
    for r in range(31):
        put_row(
            p_ref, q_ref, r, f_ref[r].astype(F32),
            left[0, r : r + 1], left[1, r : r + 1], right[r : r + 1],
        )
    layer_one(p_ref, q_ref, l_ref, w1, b1, ((0, 29, 0),), where_ref[1] == 0, {})
    rim_ref[:, 0] = l_ref[:, 0]
    rim_ref[:, 1] = l_ref[:, 28]
    layer = layer_two(l_ref, w2, b2, INNER)
    tiles = zip(quad_tiles(layer, (0, 1, 2, 3)), quad_tiles(layer, (4, 5, 6, 7)), strict=True)
    for group, pair in enumerate(tiles):
        msg_ref[group] = jnp.concatenate(pair, axis=0).astype(BF)
    copy = pltpu.make_async_copy(msg_ref, out_ref.at[:, 0:48], sem)
    copy.start()
    tiles = zip(
        quad_tiles(layer, (8, 9, 10, 11)), quad_tiles(layer, (12, 13, None, None)), strict=True
    )
    for group, pair in enumerate(tiles):
        tail_ref[group] = jnp.concatenate(pair, axis=0).astype(BF)
    copy.wait()


def side_rows(
    where_ref, cb_ref, ca_ref, r_ref, w1, b1, w2, b2, f_ref, rim_ref, p_ref, q_ref, l_ref, is_top
):
    left, right = col_halo(where_ref, ca_ref, cb_ref)
    end = r_ref[HALO * COLS : SLAB].astype(F32)

    def own(r):
        return (
            f_ref[r].astype(F32), left[0, r : r + 1], left[1, r : r + 1], right[r : r + 1]
        )

    def halo(k):
        return (
            r_ref[k * COLS : (k + 1) * COLS].astype(F32),
            end[k : k + 1], end[HALO + k : HALO + k + 1], end[2 * HALO + k : 2 * HALO + k + 1],
        )

    above = [halo(k) for k in range(4)] + [own(0), own(1)]
    below = [own(ROWS - 3 + k) for k in range(3)] + [halo(k) for k in range(3)]
    for slot, (top, bottom) in enumerate(zip(above, below, strict=True)):
        parts = [jnp.where(is_top, x, y) for x, y in zip(top, bottom, strict=True)]
        put_row(p_ref, q_ref, slot, *parts)
    l_ref[:, 0] = rim_ref[:, 1]
    l_ref[:, 5] = rim_ref[:, 0]
    off_top = jnp.logical_and(is_top, where_ref[0] == 0)
    off_bottom = jnp.logical_and(jnp.logical_not(is_top), where_ref[0] == where_ref[2] - 1)
    dead = {1: off_top, 2: off_top, 3: jnp.logical_or(off_top, off_bottom), 4: off_bottom}
    layer_one(p_ref, q_ref, l_ref, w1, b1, ((0, 4, 1),), where_ref[1] == 0, dead)
    base = jnp.where(is_top, 1, 0)
    layer = layer_two(l_ref, w2, b2, (base, base + 2))
    at = lax.broadcasted_iota(jnp.int32, layer.shape, 0) // COLS2
    gone = jnp.logical_or(
        jnp.logical_and(at == 0, off_top), jnp.logical_and(at == 1, off_bottom)
    )
    return jnp.where(gone, 0.0, layer)


def even_kernel(
    where_ref, cb_ref, ca_ref, ra_ref, w1, b1, w2, b2, f_ref, rim_ref, tail_ref, inner_hbm,
    out_ref, msg_ref, p_ref, q_ref, l_ref, sem,
):
    del inner_hbm
    layer = side_rows(
        where_ref, cb_ref, ca_ref, ra_ref, w1, b1, w2, b2, f_ref, rim_ref, p_ref, q_ref, l_ref,
        where_ref[0] % 2 == 1,
    )
    for group, tile in enumerate(quad_tiles(layer, (None, None, 0, 1))):
        tail = tail_ref[group].astype(F32)
        msg_ref[group] = jnp.concatenate(
            [tail[0:COLS2], tail[COLS2:] + tile], axis=0
        ).astype(BF)
    copy = pltpu.make_async_copy(msg_ref, out_ref.at[:, 48:96], sem)
    copy.start()
    copy.wait()


def odd_kernel(
    where_ref, cb_ref, ca_ref, rb_ref, w1, b1, w2, b2, f_ref, rim_ref, inner_hbm,
    out_ref, msg_ref, p_ref, q_ref, l_ref, sem,
):
    del inner_hbm
    layer = side_rows(
        where_ref, cb_ref, ca_ref, rb_ref, w1, b1, w2, b2, f_ref, rim_ref, p_ref, q_ref, l_ref,
        where_ref[0] % 2 == 0,
    )
    low = lax.broadcasted_iota(jnp.int32, (COLS2, 128), 1) < 64
    for group, tile in enumerate(quad_tiles(layer, (0, 1, None, None))):
        folded = pltpu.roll(pltpu.roll(tile, 64, 1), COLS2 // 2, 0)
        msg_ref[group] = jnp.where(low, tile, folded)[0:16].astype(BF)
    copy = pltpu.make_async_copy(msg_ref, out_ref.at[:, 96:DEPTH], sem)
    copy.start()
    copy.wait()


LOW = tuple(tuple(range(1, 9)) + (13, 14) + end for end in ((15, 16, -1, 0), (-1, 0, 15, 16)))
HIGH = tuple(tuple(range(5, 15)) + end for end in ((15, 16, -1, 0), (-1, 0, 15, 16)))
SLOTS = 16


def spread_kernel(where_ref, w_ref, low_ref, high_ref):
    shape = (GW, 8 * GW)
    turn = lax.broadcasted_iota(jnp.int32, shape, 1) % GW == lax.broadcasted_iota(jnp.int32, shape, 0)
    wide = jnp.dot(w_ref[...], turn.astype(BF), preferred_element_type=F32)
    lane = lax.broadcasted_iota(jnp.int32, shape, 1) // GW
    odd_row = where_ref[0] % 2 == 1

    def band(row, b, half):
        tile = jnp.zeros(shape, F32)
        for a in range(3):
            out = row + 1 - a - 8 * half
            if 0 <= out < 8:
                at = (3 * a + b) * GW
                tile = jnp.where(lane == out, wide[at : at + GW], tile)
        return tile

    for half, (rows, ref) in enumerate(((LOW, low_ref), (HIGH, high_ref))):
        for b in range(3):
            for slot, (even, odd) in enumerate(zip(*rows, strict=True)):
                tile = band(even, b, half)
                if even != odd:
                    tile = jnp.where(odd_row, band(odd, b, half), tile)
                ref[b, slot * GW : (slot + 1) * GW] = tile.astype(BF)
            ref[b, len(rows[0]) * GW :] = jnp.zeros(((SLOTS - len(rows[0])) * GW, 8 * GW), BF)


def grouped_kernel(x_ref, low_ref, high_ref, bias_ref, out_ref, held_ref, res_ref, sems):
    groups = x_ref.shape[0]
    cols = groups * COLS2
    half_row = lax.broadcasted_iota(jnp.int32, (COLS2, 128), 0) < COLS2 // 2
    for pair in range(groups // 2):
        blocks = [[] for _ in range(5)]
        for source in (2 * pair, 2 * pair + 1):
            held = x_ref[source].astype(F32)
            for quad in range(4):
                blocks[quad].append(held[quad * COLS2 : (quad + 1) * COLS2])
            folded = jnp.concatenate([held[96:DEPTH], held[96:104]], axis=0)
            turned = pltpu.roll(pltpu.roll(folded, 64, 1), COLS2 // 2, 0)
            blocks[4].append(jnp.where(half_row, folded, turned))
        for quad, parts in enumerate(blocks):
            held_ref[pair * 2 * COLS2 : (pair + 1) * 2 * COLS2, quad * 128 : (quad + 1) * 128] = (
                jnp.concatenate(parts, axis=0).astype(BF)
            )
    at = lax.broadcasted_iota(jnp.int32, (cols, 8 * GW), 0)
    copies = []
    for half, ref in enumerate((low_ref, high_ref)):
        if half == 0:
            x = jnp.concatenate([held_ref[:, 0:256], held_ref[:, 384:640]], axis=1)
        else:
            x = held_ref[:, 128:640]
        before, here, after = (
            jnp.dot(x, ref[b], preferred_element_type=F32) for b in range(3)
        )
        total = here + bias_ref[...]
        total = total + jnp.where(at == 0, 0.0, pltpu.roll(before, 1, 0))
        total = total + jnp.where(at == cols - 1, 0.0, pltpu.roll(after, cols - 1, 0))
        for part in range(2):
            piece = 2 * half + part
            res_ref[piece] = total[:, 128 * part : 128 * part + 128].T.astype(BF)
            copies.append(
                pltpu.make_async_copy(
                    res_ref.at[piece], out_ref.at[128 * piece : 128 * piece + 128], sems.at[piece]
                )
            )
            copies[-1].start()
    for copy in copies:
        copy.wait()


def on_device(features, conv_one, bias_one, conv_two, bias_two, conv_three, bias_three):
    row, col = lax.axis_index("row"), lax.axis_index("col")
    row_count, col_count = lax.axis_size("row"), lax.axis_size("col")
    where = jnp.stack([row, col, jnp.int32(row_count)]).astype(jnp.int32)
    low, high = pl.pallas_call(
        spread_kernel,
        out_shape=(
            jax.ShapeDtypeStruct((3, SLOTS * GW, 8 * GW), BF),
            jax.ShapeDtypeStruct((3, SLOTS * GW, 8 * GW), BF),
        ),
        in_specs=[SMEM, VMEM],
        out_specs=(VMEM, VMEM),
        compiler_params=PARAMS,
        name="spread_weights",
    )(where, conv_three.reshape(9 * GW, GW))
    w1, b1 = conv_one.reshape(9 * C1, C1), bias_one.reshape(1, C1)
    w2, b2 = conv_two.reshape(9 * C1, C2), bias_two.reshape(1, C2)
    b3 = jnp.tile(bias_three, 8).reshape(1, 8 * GW)

    first = jnp.transpose(features[:, :2], (1, 0, 2))
    last = jnp.transpose(features[:, COLS - 2 :], (1, 0, 2))
    odd_col = col % 2 == 1
    ca = lax.ppermute(jnp.where(odd_col, first, last), "col", pairs_even(col_count))
    cb = lax.ppermute(jnp.where(odd_col, last, first), "col", pairs_odd(col_count))
    parity = pl.pallas_call(
        parity_kernel,
        out_shape=jax.ShapeDtypeStruct((8, 128), jnp.int32),
        in_specs=[SMEM],
        out_specs=VMEM,
        compiler_params=PARAMS,
        cost_estimate=LONG,
        name="row_parity",
    )(where)

    slab = jax.ShapeDtypeStruct((SLAB, C1), BF)
    message = jax.ShapeDtypeStruct((16, DEPTH, 128), BF)
    sa, sb = pl.pallas_call(
        slab_kernel,
        out_shape=(slab, slab),
        in_specs=[SMEM, VMEM, VMEM, VMEM, VMEM],
        out_specs=(VMEM, VMEM),
        compiler_params=PARAMS,
        cost_estimate=LONG,
        name="row_slabs",
    )(where, features, cb, ca, parity)
    ra = lax.ppermute(sa, "row", pairs_even(row_count))
    rb = lax.ppermute(sb, "row", pairs_odd(row_count))
    inner, tail, rim = pl.pallas_call(
        inner_kernel,
        out_shape=(
            message,
            jax.ShapeDtypeStruct((16, 48, 128), BF),
            jax.ShapeDtypeStruct((2, 2, 56, 128), F32),
        ),
        in_specs=[SMEM] + [VMEM] * 7,
        out_specs=(HBM, VMEM, VMEM),
        scratch_shapes=[
            pltpu.VMEM((16, 48, 128), BF),
            pltpu.VMEM((3, 31, COLS, C1), BF),
            pltpu.VMEM((3, 32, C1), F32),
            pltpu.VMEM((2, 29, 56, 128), F32),
            pltpu.SemaphoreType.DMA,
        ],
        compiler_params=PARAMS,
        cost_estimate=pl.CostEstimate(
            flops=2 * 9 * C1 * (29 * 48 * C1 + 14 * 24 * C2), bytes_accessed=6_000_000, transcendentals=0
        ),
        name="inner_rows",
    )(where, features, cb, ca, w1, b1, w2, b2)
    sides = [
        pltpu.VMEM((3, 6, COLS, C1), BF),
        pltpu.VMEM((3, 8, C1), F32),
        pltpu.VMEM((2, 6, 56, 128), F32),
        pltpu.SemaphoreType.DMA,
    ]
    cost = pl.CostEstimate(
        flops=2 * 9 * C1 * (4 * 48 * C1 + 2 * 24 * C2), bytes_accessed=4_000_000, transcendentals=0
    )
    sent = pl.pallas_call(
        even_kernel,
        out_shape=message,
        in_specs=[SMEM] + [VMEM] * 10 + [HBM],
        out_specs=HBM,
        input_output_aliases={11: 0},
        scratch_shapes=[pltpu.VMEM((16, 48, 128), BF)] + sides,
        compiler_params=PARAMS,
        cost_estimate=cost,
        name="even_side",
    )(where, cb, ca, ra, w1, b1, w2, b2, features, rim, tail, inner)
    sent = pl.pallas_call(
        odd_kernel,
        out_shape=message,
        in_specs=[SMEM] + [VMEM] * 9 + [HBM],
        out_specs=HBM,
        input_output_aliases={10: 0},
        scratch_shapes=[pltpu.VMEM((16, 16, 128), BF)] + sides,
        compiler_params=PARAMS,
        cost_estimate=cost,
        name="odd_side",
    )(where, cb, ca, rb, w1, b1, w2, b2, features, rim, sent)
    x = lax.all_to_all(sent, "col", 0, 0, tiled=True)
    out = pl.pallas_call(
        grouped_kernel,
        out_shape=jax.ShapeDtypeStruct((16 * GW, 16 * COLS2), BF),
        in_specs=[VMEM] * 4,
        out_specs=HBM,
        scratch_shapes=[
            pltpu.VMEM((16 * COLS2, 640), BF),
            pltpu.VMEM((4, 4 * GW, 16 * COLS2), BF),
            pltpu.SemaphoreType.DMA((4,)),
        ],
        compiler_params=PARAMS,
        name="grouped",
    )(x, low, high, b3)
    return out.reshape(16, GW, 16 * COLS2)


def solution(mesh):
    in_specs = (
        P("row", "col", None),
        P(),
        P(),
        P(),
        P(),
        P("col", None, None, None, None),
        P("col"),
    )
    out_specs = P("row", "col", None)
    return jax.shard_map(
        on_device, mesh=mesh, in_specs=in_specs, out_specs=out_specs, check_vma=False
    )
```

```python
import functools

import jax
import jax.numpy as jnp
from jax import lax
from jax.experimental import pallas as pl
from jax.experimental.pallas import tpu as pltpu
from jax.sharding import PartitionSpec as P

BF = jnp.bfloat16
F32 = jnp.float32
ROWS, COLS, C1 = 32, 48, 256
C2, GW = 512, 32
COLS2 = COLS // 2
HALO = 4
SLAB = 208
INNER = tuple(range(0, 28, 2))
DEPTH = 112
VMEM = pl.BlockSpec(memory_space=pltpu.VMEM)
HBM = pl.BlockSpec(memory_space=pltpu.HBM)
SMEM = pl.BlockSpec(memory_space=pltpu.SMEM)
PARAMS = pltpu.CompilerParams(vmem_limit_bytes=24 * 1024 * 1024)
LONG = pl.CostEstimate(flops=10_000_000_000, bytes_accessed=1_000_000, transcendentals=0)


def pairs_even(count):
    return [(i, i ^ 1) for i in range(count)]


def pairs_odd(count):
    return [(i, ((i + 1) ^ 1) - 1) for i in range(1, count - 1)]


def put_row(p_ref, q_ref, slot, row, left2, left1, right):
    at = lax.broadcasted_iota(jnp.int32, row.shape, 0)
    p_ref[0, slot] = jnp.where(at == 0, left1, pltpu.roll(row, 1, 0)).astype(BF)
    p_ref[1, slot] = row.astype(BF)
    p_ref[2, slot] = jnp.where(at == COLS - 1, right, pltpu.roll(row, COLS - 1, 0)).astype(BF)
    q_ref[0, slot : slot + 1] = left2
    q_ref[1, slot : slot + 1] = left1
    q_ref[2, slot : slot + 1] = row[0:1]


def layer_one(p_ref, q_ref, l_ref, w1, b1, spans, first_col, dead_rows):
    total = sum(count for _, count, _ in spans)
    wide = -(-total // 16) * 16
    taps = [(a, b) for a in range(3) for b in range(3)]
    main = jnp.concatenate(
        [
            jnp.concatenate(
                [p_ref[b, at + a : at + a + count].reshape(count * COLS, C1) for a, b in taps], axis=1
            )
            for at, count, _ in spans
        ],
        axis=0,
    )
    rest = [jnp.zeros((wide - total, C1), F32)] if wide > total else []
    edge = jnp.concatenate(
        [
            jnp.concatenate(
                [q_ref[b, at + a : at + a + count] for at, count, _ in spans] + rest, axis=0
            ).astype(BF)
            for a, b in taps
        ],
        axis=1,
    )
    summed = jnp.dot(
        jnp.concatenate([main, edge], axis=0), w1[...], preferred_element_type=F32
    )
    summed = jnp.maximum(summed + b1[...], 0.0)
    done = 0
    for _, count, to in spans:
        for row in range(to, to + count):
            line = summed[done * COLS : (done + 1) * COLS]
            lead = summed[total * COLS + done : total * COLS + done + 1]
            lead = jnp.where(first_col, 0.0, lead)
            if row in dead_rows:
                line = jnp.where(dead_rows[row], 0.0, line)
                lead = jnp.where(dead_rows[row], 0.0, lead)
            for half in range(2):
                lanes = slice(128 * half, 128 * half + 128)
                l_ref[half, row, 8 : 8 + COLS] = line[:, lanes]
                l_ref[half, row, 7:8] = lead[:, lanes]
            done += 1


def layer_two(l_ref, w2, b2, bases):
    windows = [
        jnp.concatenate(
            [l_ref[half, base + a, pl.ds(7 + b, COLS2, stride=2), :] for base in bases], axis=0
        ).astype(BF)
        for a in range(3)
        for b in range(3)
        for half in range(2)
    ]
    summed = jnp.dot(jnp.concatenate(windows, axis=1), w2[...], preferred_element_type=F32)
    return jnp.maximum(summed + b2[...], 0.0)


def quad_tiles(layer, rows):
    lane = lax.broadcasted_iota(jnp.int32, (COLS2, 128), 1) // GW
    tiles = []
    for block in range(C2 // 128):
        turned = {}
        for slot, row in enumerate(rows):
            if row is not None:
                part = layer[row * COLS2 : (row + 1) * COLS2, block * 128 : (block + 1) * 128]
                turned[slot] = [part] + [pltpu.roll(part, GW * d, 1) for d in range(1, 4)]
        for m in range(4):
            tile = jnp.zeros((COLS2, 128), F32)
            for slot, parts in turned.items():
                tile = jnp.where(lane == slot, parts[(slot - m) % 4], tile)
            tiles.append(tile)
    return tiles


def fill_slab(f_ref, bottom_at, left, right, out_ref, take_top):
    for k in range(HALO):
        out_ref[k * COLS : (k + 1) * COLS] = jnp.where(take_top, f_ref[k], f_ref[bottom_at + k])
    sides = [left[0], left[1], right]
    top = jnp.concatenate([s[0:HALO] for s in sides] + [left[0][0:HALO]], axis=0)
    bottom = jnp.concatenate(
        [s[ROWS - HALO : ROWS] for s in sides] + [left[0][0:HALO]], axis=0
    )
    out_ref[HALO * COLS : SLAB] = jnp.where(take_top, top, bottom).astype(BF)


def col_halo(where_ref, ca_ref, cb_ref):
    odd_col = where_ref[1] % 2 == 1
    ca = ca_ref[...].astype(F32)
    cb = cb_ref[...].astype(F32)
    return jnp.where(odd_col, ca, cb), jnp.where(odd_col, cb, ca)[0]


def parity_kernel(where_ref, out_ref):
    out_ref[...] = jnp.full(out_ref.shape, where_ref[0] % 2, jnp.int32)


def slab_kernel(where_ref, f_ref, cb_ref, ca_ref, parity_ref, sa_ref, sb_ref):
    del parity_ref
    odd_row = where_ref[0] % 2 == 1
    left, right = col_halo(where_ref, ca_ref, cb_ref)
    fill_slab(f_ref, ROWS - HALO, left, right, sa_ref, odd_row)
    fill_slab(f_ref, ROWS - HALO, left, right, sb_ref, jnp.logical_not(odd_row))


def inner_kernel(
    where_ref, f_ref, cb_ref, ca_ref, w1, b1, w2, b2,
    out_ref, tail_ref, rim_ref, msg_ref, p_ref, q_ref, l_ref, sem,
):
    left, right = col_halo(where_ref, ca_ref, cb_ref)
    for r in range(31):
        put_row(
            p_ref, q_ref, r, f_ref[r].astype(F32),
            left[0, r : r + 1], left[1, r : r + 1], right[r : r + 1],
        )
    layer_one(p_ref, q_ref, l_ref, w1, b1, ((0, 29, 0),), where_ref[1] == 0, {})
    rim_ref[:, 0] = l_ref[:, 0]
    rim_ref[:, 1] = l_ref[:, 28]
    layer = layer_two(l_ref, w2, b2, INNER)
    tiles = zip(quad_tiles(layer, (0, 1, 2, 3)), quad_tiles(layer, (4, 5, 6, 7)), strict=True)
    for group, pair in enumerate(tiles):
        msg_ref[group] = jnp.concatenate(pair, axis=0).astype(BF)
    copy = pltpu.make_async_copy(msg_ref, out_ref.at[:, 0:48], sem)
    copy.start()
    tiles = zip(
        quad_tiles(layer, (8, 9, 10, 11)), quad_tiles(layer, (12, 13, None, None)), strict=True
    )
    for group, pair in enumerate(tiles):
        tail_ref[group] = jnp.concatenate(pair, axis=0).astype(BF)
    copy.wait()


def side_rows(
    where_ref, cb_ref, ca_ref, r_ref, w1, b1, w2, b2, f_ref, rim_ref, p_ref, q_ref, l_ref, is_top
):
    left, right = col_halo(where_ref, ca_ref, cb_ref)
    end = r_ref[HALO * COLS : SLAB].astype(F32)

    def own(r):
        return (
            f_ref[r].astype(F32), left[0, r : r + 1], left[1, r : r + 1], right[r : r + 1]
        )

    def halo(k):
        return (
            r_ref[k * COLS : (k + 1) * COLS].astype(F32),
            end[k : k + 1], end[HALO + k : HALO + k + 1], end[2 * HALO + k : 2 * HALO + k + 1],
        )

    above = [halo(k) for k in range(4)] + [own(0), own(1)]
    below = [own(ROWS - 3 + k) for k in range(3)] + [halo(k) for k in range(3)]
    for slot, (top, bottom) in enumerate(zip(above, below, strict=True)):
        parts = [jnp.where(is_top, x, y) for x, y in zip(top, bottom, strict=True)]
        put_row(p_ref, q_ref, slot, *parts)
    l_ref[:, 0] = rim_ref[:, 1]
    l_ref[:, 5] = rim_ref[:, 0]
    off_top = jnp.logical_and(is_top, where_ref[0] == 0)
    off_bottom = jnp.logical_and(jnp.logical_not(is_top), where_ref[0] == where_ref[2] - 1)
    dead = {1: off_top, 2: off_top, 3: jnp.logical_or(off_top, off_bottom), 4: off_bottom}
    layer_one(p_ref, q_ref, l_ref, w1, b1, ((0, 4, 1),), where_ref[1] == 0, dead)
    base = jnp.where(is_top, 1, 0)
    layer = layer_two(l_ref, w2, b2, (base, base + 2))
    at = lax.broadcasted_iota(jnp.int32, layer.shape, 0) // COLS2
    gone = jnp.logical_or(
        jnp.logical_and(at == 0, off_top), jnp.logical_and(at == 1, off_bottom)
    )
    return jnp.where(gone, 0.0, layer)


def even_kernel(
    where_ref, cb_ref, ca_ref, ra_ref, w1, b1, w2, b2, f_ref, rim_ref, tail_ref, inner_hbm,
    out_ref, msg_ref, p_ref, q_ref, l_ref, sem,
):
    del inner_hbm
    layer = side_rows(
        where_ref, cb_ref, ca_ref, ra_ref, w1, b1, w2, b2, f_ref, rim_ref, p_ref, q_ref, l_ref,
        where_ref[0] % 2 == 1,
    )
    for group, tile in enumerate(quad_tiles(layer, (None, None, 0, 1))):
        tail = tail_ref[group].astype(F32)
        msg_ref[group] = jnp.concatenate(
            [tail[0:COLS2], tail[COLS2:] + tile], axis=0
        ).astype(BF)
    copy = pltpu.make_async_copy(msg_ref, out_ref.at[:, 48:96], sem)
    copy.start()
    copy.wait()


def odd_kernel(
    where_ref, cb_ref, ca_ref, rb_ref, w1, b1, w2, b2, f_ref, rim_ref, inner_hbm,
    out_ref, msg_ref, p_ref, q_ref, l_ref, sems,
):
    del inner_hbm
    layer = side_rows(
        where_ref, cb_ref, ca_ref, rb_ref, w1, b1, w2, b2, f_ref, rim_ref, p_ref, q_ref, l_ref,
        where_ref[0] % 2 == 0,
    )
    low = lax.broadcasted_iota(jnp.int32, (COLS2, 128), 1) < 64
    copies = []
    for group, tile in enumerate(quad_tiles(layer, (0, 1, None, None))):
        folded = pltpu.roll(pltpu.roll(tile, 64, 1), COLS2 // 2, 0)
        msg_ref[group] = jnp.where(low, tile, folded)[0:16].astype(BF)
        if group % 8 == 7:
            part = slice(group - 7, group + 1)
            copies.append(
                pltpu.make_async_copy(
                    msg_ref.at[part], out_ref.at[part, 96:DEPTH], sems.at[group // 8]
                )
            )
            copies[-1].start()
    for copy in copies:
        copy.wait()


LOW = tuple(tuple(range(1, 9)) + (13, 14) + end for end in ((15, 16, -1, 0), (-1, 0, 15, 16)))
HIGH = tuple(tuple(range(5, 15)) + end for end in ((15, 16, -1, 0), (-1, 0, 15, 16)))
SLOTS = 16


def spread_kernel(where_ref, w_ref, low_ref, high_ref):
    shape = (GW, 8 * GW)
    turn = lax.broadcasted_iota(jnp.int32, shape, 1) % GW == lax.broadcasted_iota(jnp.int32, shape, 0)
    wide = jnp.dot(w_ref[...], turn.astype(BF), preferred_element_type=F32)
    lane = lax.broadcasted_iota(jnp.int32, shape, 1) // GW
    odd_row = where_ref[0] % 2 == 1

    def band(row, b, half):
        tile = jnp.zeros(shape, F32)
        for a in range(3):
            out = row + 1 - a - 8 * half
            if 0 <= out < 8:
                at = (3 * a + b) * GW
                tile = jnp.where(lane == out, wide[at : at + GW], tile)
        return tile

    for half, (rows, ref) in enumerate(((LOW, low_ref), (HIGH, high_ref))):
        for b in range(3):
            for slot, (even, odd) in enumerate(zip(*rows, strict=True)):
                tile = band(even, b, half)
                if even != odd:
                    tile = jnp.where(odd_row, band(odd, b, half), tile)
                ref[b, slot * GW : (slot + 1) * GW] = tile.astype(BF)
            ref[b, len(rows[0]) * GW :] = jnp.zeros(((SLOTS - len(rows[0])) * GW, 8 * GW), BF)


def grouped_kernel(x_ref, low_ref, high_ref, bias_ref, out_ref, held_ref, res_ref, sems):
    groups = x_ref.shape[0]
    cols = groups * COLS2
    half_row = lax.broadcasted_iota(jnp.int32, (COLS2, 128), 0) < COLS2 // 2
    for pair in range(groups // 2):
        blocks = [[] for _ in range(5)]
        for source in (2 * pair, 2 * pair + 1):
            held = x_ref[source].astype(F32)
            for quad in range(4):
                blocks[quad].append(held[quad * COLS2 : (quad + 1) * COLS2])
            folded = jnp.concatenate([held[96:DEPTH], held[96:104]], axis=0)
            turned = pltpu.roll(pltpu.roll(folded, 64, 1), COLS2 // 2, 0)
            blocks[4].append(jnp.where(half_row, folded, turned))
        for quad, parts in enumerate(blocks):
            held_ref[pair * 2 * COLS2 : (pair + 1) * 2 * COLS2, quad * 128 : (quad + 1) * 128] = (
                jnp.concatenate(parts, axis=0).astype(BF)
            )
    at = lax.broadcasted_iota(jnp.int32, (cols, 8 * GW), 0)
    copies = []
    for half, ref in enumerate((low_ref, high_ref)):
        if half == 0:
            x = jnp.concatenate([held_ref[:, 0:256], held_ref[:, 384:640]], axis=1)
        else:
            x = held_ref[:, 128:640]
        before, here, after = (
            jnp.dot(x, ref[b], preferred_element_type=F32) for b in range(3)
        )
        total = here + bias_ref[...]
        total = total + jnp.where(at == 0, 0.0, pltpu.roll(before, 1, 0))
        total = total + jnp.where(at == cols - 1, 0.0, pltpu.roll(after, cols - 1, 0))
        for part in range(2):
            piece = 2 * half + part
            res_ref[piece] = total[:, 128 * part : 128 * part + 128].T.astype(BF)
            copies.append(
                pltpu.make_async_copy(
                    res_ref.at[piece], out_ref.at[128 * piece : 128 * piece + 128], sems.at[piece]
                )
            )
            copies[-1].start()
    for copy in copies:
        copy.wait()


def on_device(features, conv_one, bias_one, conv_two, bias_two, conv_three, bias_three):
    row, col = lax.axis_index("row"), lax.axis_index("col")
    row_count, col_count = lax.axis_size("row"), lax.axis_size("col")
    where = jnp.stack([row, col, jnp.int32(row_count)]).astype(jnp.int32)
    low, high = pl.pallas_call(
        spread_kernel,
        out_shape=(
            jax.ShapeDtypeStruct((3, SLOTS * GW, 8 * GW), BF),
            jax.ShapeDtypeStruct((3, SLOTS * GW, 8 * GW), BF),
        ),
        in_specs=[SMEM, VMEM],
        out_specs=(VMEM, VMEM),
        compiler_params=PARAMS,
        name="spread_weights",
    )(where, conv_three.reshape(9 * GW, GW))
    w1, b1 = conv_one.reshape(9 * C1, C1), bias_one.reshape(1, C1)
    w2, b2 = conv_two.reshape(9 * C1, C2), bias_two.reshape(1, C2)
    b3 = jnp.tile(bias_three, 8).reshape(1, 8 * GW)

    first = jnp.transpose(features[:, :2], (1, 0, 2))
    last = jnp.transpose(features[:, COLS - 2 :], (1, 0, 2))
    odd_col = col % 2 == 1
    cb = lax.ppermute(jnp.where(odd_col, last, first), "col", pairs_odd(col_count))
    ca = lax.ppermute(jnp.where(odd_col, first, last), "col", pairs_even(col_count))
    parity = pl.pallas_call(
        parity_kernel,
        out_shape=jax.ShapeDtypeStruct((8, 128), jnp.int32),
        in_specs=[SMEM],
        out_specs=VMEM,
        compiler_params=PARAMS,
        cost_estimate=LONG,
        name="row_parity",
    )(where)

    slab = jax.ShapeDtypeStruct((SLAB, C1), BF)
    message = jax.ShapeDtypeStruct((16, DEPTH, 128), BF)
    sa, sb = pl.pallas_call(
        slab_kernel,
        out_shape=(slab, slab),
        in_specs=[SMEM, VMEM, VMEM, VMEM, VMEM],
        out_specs=(VMEM, VMEM),
        compiler_params=PARAMS,
        cost_estimate=LONG,
        name="row_slabs",
    )(where, features, cb, ca, parity)
    ra = lax.ppermute(sa, "row", pairs_even(row_count))
    rb = lax.ppermute(sb, "row", pairs_odd(row_count))
    inner, tail, rim = pl.pallas_call(
        inner_kernel,
        out_shape=(
            message,
            jax.ShapeDtypeStruct((16, 48, 128), BF),
            jax.ShapeDtypeStruct((2, 2, 56, 128), F32),
        ),
        in_specs=[SMEM] + [VMEM] * 7,
        out_specs=(HBM, VMEM, VMEM),
        scratch_shapes=[
            pltpu.VMEM((16, 48, 128), BF),
            pltpu.VMEM((3, 31, COLS, C1), BF),
            pltpu.VMEM((3, 32, C1), F32),
            pltpu.VMEM((2, 29, 56, 128), F32),
            pltpu.SemaphoreType.DMA,
        ],
        compiler_params=PARAMS,
        cost_estimate=pl.CostEstimate(
            flops=2 * 9 * C1 * (29 * 48 * C1 + 14 * 24 * C2), bytes_accessed=6_000_000, transcendentals=0
        ),
        name="inner_rows",
    )(where, features, cb, ca, w1, b1, w2, b2)
    sides = [
        pltpu.VMEM((3, 6, COLS, C1), BF),
        pltpu.VMEM((3, 8, C1), F32),
        pltpu.VMEM((2, 6, 56, 128), F32),
    ]
    cost = pl.CostEstimate(
        flops=2 * 9 * C1 * (4 * 48 * C1 + 2 * 24 * C2), bytes_accessed=4_000_000, transcendentals=0
    )
    sent = pl.pallas_call(
        even_kernel,
        out_shape=message,
        in_specs=[SMEM] + [VMEM] * 10 + [HBM],
        out_specs=HBM,
        input_output_aliases={11: 0},
        scratch_shapes=[pltpu.VMEM((16, 48, 128), BF)] + sides + [pltpu.SemaphoreType.DMA],
        compiler_params=PARAMS,
        cost_estimate=cost,
        name="even_side",
    )(where, cb, ca, ra, w1, b1, w2, b2, features, rim, tail, inner)
    sent = pl.pallas_call(
        odd_kernel,
        out_shape=message,
        in_specs=[SMEM] + [VMEM] * 9 + [HBM],
        out_specs=HBM,
        input_output_aliases={10: 0},
        scratch_shapes=[pltpu.VMEM((16, 16, 128), BF)] + sides + [pltpu.SemaphoreType.DMA((2,))],
        compiler_params=PARAMS,
        cost_estimate=cost,
        name="odd_side",
    )(where, cb, ca, rb, w1, b1, w2, b2, features, rim, sent)
    x = lax.all_to_all(sent, "col", 0, 0, tiled=True)
    out = pl.pallas_call(
        grouped_kernel,
        out_shape=jax.ShapeDtypeStruct((16 * GW, 16 * COLS2), BF),
        in_specs=[VMEM] * 4,
        out_specs=HBM,
        scratch_shapes=[
            pltpu.VMEM((16 * COLS2, 640), BF),
            pltpu.VMEM((4, 4 * GW, 16 * COLS2), BF),
            pltpu.SemaphoreType.DMA((4,)),
        ],
        compiler_params=PARAMS,
        name="grouped",
    )(x, low, high, b3)
    return out.reshape(16, GW, 16 * COLS2)


def solution(mesh):
    in_specs = (
        P("row", "col", None),
        P(),
        P(),
        P(),
        P(),
        P("col", None, None, None, None),
        P("col"),
    )
    out_specs = P("row", "col", None)
    return jax.shard_map(
        on_device, mesh=mesh, in_specs=in_specs, out_specs=out_specs, check_vma=False
    )
```

```python
import functools

import jax
import jax.numpy as jnp
from jax import lax
from jax.experimental import pallas as pl
from jax.experimental.pallas import tpu as pltpu
from jax.sharding import PartitionSpec as P

BF = jnp.bfloat16
F32 = jnp.float32
ROWS, COLS, C1 = 32, 48, 256
C2, GW = 512, 32
COLS2 = COLS // 2
HALO = 4
SLAB = 208
INNER = tuple(range(0, 28, 2))
DEPTH = 112
VMEM = pl.BlockSpec(memory_space=pltpu.VMEM)
HBM = pl.BlockSpec(memory_space=pltpu.HBM)
SMEM = pl.BlockSpec(memory_space=pltpu.SMEM)
PARAMS = pltpu.CompilerParams(vmem_limit_bytes=24 * 1024 * 1024)
LONG = pl.CostEstimate(flops=10_000_000_000, bytes_accessed=1_000_000, transcendentals=0)


def pairs_even(count):
    return [(i, i ^ 1) for i in range(count)]


def pairs_odd(count):
    return [(i, ((i + 1) ^ 1) - 1) for i in range(1, count - 1)]


def put_row(p_ref, q_ref, slot, row, left2, left1, right):
    at = lax.broadcasted_iota(jnp.int32, row.shape, 0)
    p_ref[0, slot] = jnp.where(at == 0, left1, pltpu.roll(row, 1, 0)).astype(BF)
    p_ref[1, slot] = row.astype(BF)
    p_ref[2, slot] = jnp.where(at == COLS - 1, right, pltpu.roll(row, COLS - 1, 0)).astype(BF)
    q_ref[0, slot : slot + 1] = left2
    q_ref[1, slot : slot + 1] = left1
    q_ref[2, slot : slot + 1] = row[0:1]


def layer_one(p_ref, q_ref, l_ref, w1, b1, spans, first_col, dead_rows):
    total = sum(count for _, count, _ in spans)
    wide = -(-total // 16) * 16
    taps = [(a, b) for a in range(3) for b in range(3)]
    main = jnp.concatenate(
        [
            jnp.concatenate(
                [p_ref[b, at + a : at + a + count].reshape(count * COLS, C1) for a, b in taps], axis=1
            )
            for at, count, _ in spans
        ],
        axis=0,
    )
    rest = [jnp.zeros((wide - total, C1), F32)] if wide > total else []
    edge = jnp.concatenate(
        [
            jnp.concatenate(
                [q_ref[b, at + a : at + a + count] for at, count, _ in spans] + rest, axis=0
            ).astype(BF)
            for a, b in taps
        ],
        axis=1,
    )
    summed = jnp.dot(
        jnp.concatenate([main, edge], axis=0), w1[...], preferred_element_type=F32
    )
    summed = jnp.maximum(summed + b1[...], 0.0)
    done = 0
    for _, count, to in spans:
        for row in range(to, to + count):
            line = summed[done * COLS : (done + 1) * COLS]
            lead = summed[total * COLS + done : total * COLS + done + 1]
            lead = jnp.where(first_col, 0.0, lead)
            if row in dead_rows:
                line = jnp.where(dead_rows[row], 0.0, line)
                lead = jnp.where(dead_rows[row], 0.0, lead)
            for half in range(2):
                lanes = slice(128 * half, 128 * half + 128)
                l_ref[half, row, 8 : 8 + COLS] = line[:, lanes]
                l_ref[half, row, 7:8] = lead[:, lanes]
            done += 1


def layer_two(l_ref, w2, b2, bases):
    windows = [
        jnp.concatenate(
            [l_ref[half, base + a, pl.ds(7 + b, COLS2, stride=2), :] for base in bases], axis=0
        ).astype(BF)
        for a in range(3)
        for b in range(3)
        for half in range(2)
    ]
    summed = jnp.dot(jnp.concatenate(windows, axis=1), w2[...], preferred_element_type=F32)
    return jnp.maximum(summed + b2[...], 0.0)


def quad_tiles(layer, rows):
    lane = lax.broadcasted_iota(jnp.int32, (COLS2, 128), 1) // GW
    tiles = []
    for block in range(C2 // 128):
        turned = {}
        for slot, row in enumerate(rows):
            if row is not None:
                part = layer[row * COLS2 : (row + 1) * COLS2, block * 128 : (block + 1) * 128]
                turned[slot] = [part] + [pltpu.roll(part, GW * d, 1) for d in range(1, 4)]
        for m in range(4):
            tile = jnp.zeros((COLS2, 128), F32)
            for slot, parts in turned.items():
                tile = jnp.where(lane == slot, parts[(slot - m) % 4], tile)
            tiles.append(tile)
    return tiles


def fill_slab(f_ref, bottom_at, left, right, out_ref, take_top):
    for k in range(HALO):
        out_ref[k * COLS : (k + 1) * COLS] = jnp.where(take_top, f_ref[k], f_ref[bottom_at + k])
    sides = [left[0], left[1], right]
    top = jnp.concatenate([s[0:HALO] for s in sides] + [left[0][0:HALO]], axis=0)
    bottom = jnp.concatenate(
        [s[ROWS - HALO : ROWS] for s in sides] + [left[0][0:HALO]], axis=0
    )
    out_ref[HALO * COLS : SLAB] = jnp.where(take_top, top, bottom).astype(BF)


def col_halo(where_ref, ca_ref, cb_ref):
    odd_col = where_ref[1] % 2 == 1
    ca = ca_ref[...].astype(F32)
    cb = cb_ref[...].astype(F32)
    return jnp.where(odd_col, ca, cb), jnp.where(odd_col, cb, ca)[0]


def parity_kernel(where_ref, out_ref):
    out_ref[...] = jnp.full(out_ref.shape, where_ref[0] % 2, jnp.int32)


def slab_kernel(where_ref, f_ref, cb_ref, ca_ref, parity_ref, sa_ref, sb_ref):
    del parity_ref
    odd_row = where_ref[0] % 2 == 1
    left, right = col_halo(where_ref, ca_ref, cb_ref)
    fill_slab(f_ref, ROWS - HALO, left, right, sa_ref, odd_row)
    fill_slab(f_ref, ROWS - HALO, left, right, sb_ref, jnp.logical_not(odd_row))


def inner_kernel(
    where_ref, f_ref, cb_ref, ca_ref, w1, b1, w2, b2,
    out_ref, tail_ref, rim_ref, msg_ref, p_ref, q_ref, l_ref, sem,
):
    left, right = col_halo(where_ref, ca_ref, cb_ref)
    done = 0
    for at, count in ((0, 15), (15, 14)):
        for r in range(done, at + count + 2):
            put_row(
                p_ref, q_ref, r, f_ref[r].astype(F32),
                left[0, r : r + 1], left[1, r : r + 1], right[r : r + 1],
            )
        done = at + count + 2
        layer_one(p_ref, q_ref, l_ref, w1, b1, ((at, count, at),), where_ref[1] == 0, {})
    rim_ref[:, 0] = l_ref[:, 0]
    rim_ref[:, 1] = l_ref[:, 28]
    layer = layer_two(l_ref, w2, b2, INNER)
    tiles = zip(quad_tiles(layer, (0, 1, 2, 3)), quad_tiles(layer, (4, 5, 6, 7)), strict=True)
    for group, pair in enumerate(tiles):
        msg_ref[group] = jnp.concatenate(pair, axis=0).astype(BF)
    copy = pltpu.make_async_copy(msg_ref, out_ref.at[:, 0:48], sem)
    copy.start()
    tiles = zip(
        quad_tiles(layer, (8, 9, 10, 11)), quad_tiles(layer, (12, 13, None, None)), strict=True
    )
    for group, pair in enumerate(tiles):
        tail_ref[group] = jnp.concatenate(pair, axis=0).astype(BF)
    copy.wait()


def side_rows(
    where_ref, cb_ref, ca_ref, r_ref, w1, b1, w2, b2, f_ref, rim_ref, p_ref, q_ref, l_ref, is_top
):
    left, right = col_halo(where_ref, ca_ref, cb_ref)
    end = r_ref[HALO * COLS : SLAB].astype(F32)

    def own(r):
        return (
            f_ref[r].astype(F32), left[0, r : r + 1], left[1, r : r + 1], right[r : r + 1]
        )

    def halo(k):
        return (
            r_ref[k * COLS : (k + 1) * COLS].astype(F32),
            end[k : k + 1], end[HALO + k : HALO + k + 1], end[2 * HALO + k : 2 * HALO + k + 1],
        )

    above = [halo(k) for k in range(4)] + [own(0), own(1)]
    below = [own(ROWS - 3 + k) for k in range(3)] + [halo(k) for k in range(3)]
    for slot, (top, bottom) in enumerate(zip(above, below, strict=True)):
        parts = [jnp.where(is_top, x, y) for x, y in zip(top, bottom, strict=True)]
        put_row(p_ref, q_ref, slot, *parts)
    l_ref[:, 0] = rim_ref[:, 1]
    l_ref[:, 5] = rim_ref[:, 0]
    off_top = jnp.logical_and(is_top, where_ref[0] == 0)
    off_bottom = jnp.logical_and(jnp.logical_not(is_top), where_ref[0] == where_ref[2] - 1)
    dead = {1: off_top, 2: off_top, 3: jnp.logical_or(off_top, off_bottom), 4: off_bottom}
    layer_one(p_ref, q_ref, l_ref, w1, b1, ((0, 4, 1),), where_ref[1] == 0, dead)
    base = jnp.where(is_top, 1, 0)
    layer = layer_two(l_ref, w2, b2, (base, base + 2))
    at = lax.broadcasted_iota(jnp.int32, layer.shape, 0) // COLS2
    gone = jnp.logical_or(
        jnp.logical_and(at == 0, off_top), jnp.logical_and(at == 1, off_bottom)
    )
    return jnp.where(gone, 0.0, layer)


def even_kernel(
    where_ref, cb_ref, ca_ref, ra_ref, w1, b1, w2, b2, f_ref, rim_ref, tail_ref, inner_hbm,
    out_ref, msg_ref, p_ref, q_ref, l_ref, sem,
):
    del inner_hbm
    layer = side_rows(
        where_ref, cb_ref, ca_ref, ra_ref, w1, b1, w2, b2, f_ref, rim_ref, p_ref, q_ref, l_ref,
        where_ref[0] % 2 == 1,
    )
    for group, tile in enumerate(quad_tiles(layer, (None, None, 0, 1))):
        tail = tail_ref[group].astype(F32)
        msg_ref[group] = jnp.concatenate(
            [tail[0:COLS2], tail[COLS2:] + tile], axis=0
        ).astype(BF)
    copy = pltpu.make_async_copy(msg_ref, out_ref.at[:, 48:96], sem)
    copy.start()
    copy.wait()


def odd_kernel(
    where_ref, cb_ref, ca_ref, rb_ref, w1, b1, w2, b2, f_ref, rim_ref, inner_hbm,
    out_ref, msg_ref, p_ref, q_ref, l_ref, sem,
):
    del inner_hbm
    layer = side_rows(
        where_ref, cb_ref, ca_ref, rb_ref, w1, b1, w2, b2, f_ref, rim_ref, p_ref, q_ref, l_ref,
        where_ref[0] % 2 == 0,
    )
    low = lax.broadcasted_iota(jnp.int32, (COLS2, 128), 1) < 64
    for group, tile in enumerate(quad_tiles(layer, (0, 1, None, None))):
        folded = pltpu.roll(pltpu.roll(tile, 64, 1), COLS2 // 2, 0)
        msg_ref[group] = jnp.where(low, tile, folded)[0:16].astype(BF)
    copy = pltpu.make_async_copy(msg_ref, out_ref.at[:, 96:DEPTH], sem)
    copy.start()
    copy.wait()


LOW = tuple(tuple(range(1, 9)) + (13, 14) + end for end in ((15, 16, -1, 0), (-1, 0, 15, 16)))
HIGH = tuple(tuple(range(5, 15)) + end for end in ((15, 16, -1, 0), (-1, 0, 15, 16)))
SLOTS = 16


def spread_kernel(where_ref, w_ref, low_ref, high_ref):
    shape = (GW, 8 * GW)
    turn = lax.broadcasted_iota(jnp.int32, shape, 1) % GW == lax.broadcasted_iota(jnp.int32, shape, 0)
    wide = jnp.dot(w_ref[...], turn.astype(BF), preferred_element_type=F32)
    lane = lax.broadcasted_iota(jnp.int32, shape, 1) // GW
    odd_row = where_ref[0] % 2 == 1

    def band(row, b, half):
        tile = jnp.zeros(shape, F32)
        for a in range(3):
            out = row + 1 - a - 8 * half
            if 0 <= out < 8:
                at = (3 * a + b) * GW
                tile = jnp.where(lane == out, wide[at : at + GW], tile)
        return tile

    for half, (rows, ref) in enumerate(((LOW, low_ref), (HIGH, high_ref))):
        for b in range(3):
            for slot, (even, odd) in enumerate(zip(*rows, strict=True)):
                tile = band(even, b, half)
                if even != odd:
                    tile = jnp.where(odd_row, band(odd, b, half), tile)
                ref[b, slot * GW : (slot + 1) * GW] = tile.astype(BF)
            ref[b, len(rows[0]) * GW :] = jnp.zeros(((SLOTS - len(rows[0])) * GW, 8 * GW), BF)


def grouped_kernel(x_ref, low_ref, high_ref, bias_ref, out_ref, held_ref, res_ref, sems):
    groups = x_ref.shape[0]
    cols = groups * COLS2
    half_row = lax.broadcasted_iota(jnp.int32, (COLS2, 128), 0) < COLS2 // 2
    for pair in range(groups // 2):
        blocks = [[] for _ in range(5)]
        for source in (2 * pair, 2 * pair + 1):
            held = x_ref[source].astype(F32)
            for quad in range(4):
                blocks[quad].append(held[quad * COLS2 : (quad + 1) * COLS2])
            folded = jnp.concatenate([held[96:DEPTH], held[96:104]], axis=0)
            turned = pltpu.roll(pltpu.roll(folded, 64, 1), COLS2 // 2, 0)
            blocks[4].append(jnp.where(half_row, folded, turned))
        for quad, parts in enumerate(blocks):
            held_ref[pair * 2 * COLS2 : (pair + 1) * 2 * COLS2, quad * 128 : (quad + 1) * 128] = (
                jnp.concatenate(parts, axis=0).astype(BF)
            )
    at = lax.broadcasted_iota(jnp.int32, (cols, 8 * GW), 0)
    copies = []
    for half, ref in enumerate((low_ref, high_ref)):
        if half == 0:
            x = jnp.concatenate([held_ref[:, 0:256], held_ref[:, 384:640]], axis=1)
        else:
            x = held_ref[:, 128:640]
        before, here, after = (
            jnp.dot(x, ref[b], preferred_element_type=F32) for b in range(3)
        )
        total = here + bias_ref[...]
        total = total + jnp.where(at == 0, 0.0, pltpu.roll(before, 1, 0))
        total = total + jnp.where(at == cols - 1, 0.0, pltpu.roll(after, cols - 1, 0))
        for part in range(2):
            piece = 2 * half + part
            res_ref[piece] = total[:, 128 * part : 128 * part + 128].T.astype(BF)
            copies.append(
                pltpu.make_async_copy(
                    res_ref.at[piece], out_ref.at[128 * piece : 128 * piece + 128], sems.at[piece]
                )
            )
            copies[-1].start()
    for copy in copies:
        copy.wait()


def on_device(features, conv_one, bias_one, conv_two, bias_two, conv_three, bias_three):
    row, col = lax.axis_index("row"), lax.axis_index("col")
    row_count, col_count = lax.axis_size("row"), lax.axis_size("col")
    where = jnp.stack([row, col, jnp.int32(row_count)]).astype(jnp.int32)
    low, high = pl.pallas_call(
        spread_kernel,
        out_shape=(
            jax.ShapeDtypeStruct((3, SLOTS * GW, 8 * GW), BF),
            jax.ShapeDtypeStruct((3, SLOTS * GW, 8 * GW), BF),
        ),
        in_specs=[SMEM, VMEM],
        out_specs=(VMEM, VMEM),
        compiler_params=PARAMS,
        name="spread_weights",
    )(where, conv_three.reshape(9 * GW, GW))
    w1, b1 = conv_one.reshape(9 * C1, C1), bias_one.reshape(1, C1)
    w2, b2 = conv_two.reshape(9 * C1, C2), bias_two.reshape(1, C2)
    b3 = jnp.tile(bias_three, 8).reshape(1, 8 * GW)

    first = jnp.transpose(features[:, :2], (1, 0, 2))
    last = jnp.transpose(features[:, COLS - 2 :], (1, 0, 2))
    odd_col = col % 2 == 1
    ca = lax.ppermute(jnp.where(odd_col, first, last), "col", pairs_even(col_count))
    cb = lax.ppermute(jnp.where(odd_col, last, first), "col", pairs_odd(col_count))
    parity = pl.pallas_call(
        parity_kernel,
        out_shape=jax.ShapeDtypeStruct((8, 128), jnp.int32),
        in_specs=[SMEM],
        out_specs=VMEM,
        compiler_params=PARAMS,
        cost_estimate=LONG,
        name="row_parity",
    )(where)

    slab = jax.ShapeDtypeStruct((SLAB, C1), BF)
    message = jax.ShapeDtypeStruct((16, DEPTH, 128), BF)
    sa, sb = pl.pallas_call(
        slab_kernel,
        out_shape=(slab, slab),
        in_specs=[SMEM, VMEM, VMEM, VMEM, VMEM],
        out_specs=(VMEM, VMEM),
        compiler_params=PARAMS,
        cost_estimate=LONG,
        name="row_slabs",
    )(where, features, cb, ca, parity)
    ra = lax.ppermute(sa, "row", pairs_even(row_count))
    rb = lax.ppermute(sb, "row", pairs_odd(row_count))
    inner, tail, rim = pl.pallas_call(
        inner_kernel,
        out_shape=(
            message,
            jax.ShapeDtypeStruct((16, 48, 128), BF),
            jax.ShapeDtypeStruct((2, 2, 56, 128), F32),
        ),
        in_specs=[SMEM] + [VMEM] * 7,
        out_specs=(HBM, VMEM, VMEM),
        scratch_shapes=[
            pltpu.VMEM((16, 48, 128), BF),
            pltpu.VMEM((3, 31, COLS, C1), BF),
            pltpu.VMEM((3, 32, C1), F32),
            pltpu.VMEM((2, 29, 56, 128), F32),
            pltpu.SemaphoreType.DMA,
        ],
        compiler_params=PARAMS,
        cost_estimate=pl.CostEstimate(
            flops=2 * 9 * C1 * (29 * 48 * C1 + 14 * 24 * C2), bytes_accessed=6_000_000, transcendentals=0
        ),
        name="inner_rows",
    )(where, features, cb, ca, w1, b1, w2, b2)
    sides = [
        pltpu.VMEM((3, 6, COLS, C1), BF),
        pltpu.VMEM((3, 8, C1), F32),
        pltpu.VMEM((2, 6, 56, 128), F32),
        pltpu.SemaphoreType.DMA,
    ]
    cost = pl.CostEstimate(
        flops=2 * 9 * C1 * (4 * 48 * C1 + 2 * 24 * C2), bytes_accessed=4_000_000, transcendentals=0
    )
    sent = pl.pallas_call(
        even_kernel,
        out_shape=message,
        in_specs=[SMEM] + [VMEM] * 10 + [HBM],
        out_specs=HBM,
        input_output_aliases={11: 0},
        scratch_shapes=[pltpu.VMEM((16, 48, 128), BF)] + sides,
        compiler_params=PARAMS,
        cost_estimate=cost,
        name="even_side",
    )(where, cb, ca, ra, w1, b1, w2, b2, features, rim, tail, inner)
    sent = pl.pallas_call(
        odd_kernel,
        out_shape=message,
        in_specs=[SMEM] + [VMEM] * 9 + [HBM],
        out_specs=HBM,
        input_output_aliases={10: 0},
        scratch_shapes=[pltpu.VMEM((16, 16, 128), BF)] + sides,
        compiler_params=PARAMS,
        cost_estimate=cost,
        name="odd_side",
    )(where, cb, ca, rb, w1, b1, w2, b2, features, rim, sent)
    x = lax.all_to_all(sent, "col", 0, 0, tiled=True)
    out = pl.pallas_call(
        grouped_kernel,
        out_shape=jax.ShapeDtypeStruct((16 * GW, 16 * COLS2), BF),
        in_specs=[VMEM] * 4,
        out_specs=HBM,
        scratch_shapes=[
            pltpu.VMEM((16 * COLS2, 640), BF),
            pltpu.VMEM((4, 4 * GW, 16 * COLS2), BF),
            pltpu.SemaphoreType.DMA((4,)),
        ],
        compiler_params=PARAMS,
        name="grouped",
    )(x, low, high, b3)
    return out.reshape(16, GW, 16 * COLS2)


def solution(mesh):
    in_specs = (
        P("row", "col", None),
        P(),
        P(),
        P(),
        P(),
        P("col", None, None, None, None),
        P("col"),
    )
    out_specs = P("row", "col", None)
    return jax.shard_map(
        on_device, mesh=mesh, in_specs=in_specs, out_specs=out_specs, check_vma=False
    )
```
